128 devices in a mesh: frame: 16 (over x, y_lo, core), dp: 8 (over z, y_hi).
Axes of the slice: x: 4, y: 4 (y_hi: 2, y_lo: 2; y = y_hi * 2 + y_lo), z: 4, core: 2. Of those that a mesh axis runs over, the one named last changes fastest.
Arguments:
- tokens: bfloat16 [6144, 5120], P(('frame', 'dp')), may hold values from -8 to 8
- qkv_weight: bfloat16 [5120, 3, 3072], P(None, None, 'dp'), may hold values from -0.078125 to 0.078125
- out_weight: bfloat16 [3072, 5120], P('dp'), may hold values from -0.109375 to 0.109375
- mod_table: float32 [8, 3, 5120], replicated, may hold values from -3 to 3
- levels: int32 [16], replicated, may hold values from 0 to 6
- frame_order: int32 [16], replicated, may hold values from 0 to 15, each once
Outputs:
- hidden: bfloat16 [6144, 5120], P(('frame', 'dp'))
- attended: bfloat16 [6144, 3072], P('frame', 'dp')
The draws below stay inside these ranges and needn't reach their ends.
Inputs may be any that keep to these rules, and one draw needn't show every extreme that they name: levels + 1 is a row of mod_table. frame_order names each place in time once.
All inputs are finite; a program needn't handle non-finite values.
Results may differ from the reference program's by a relative error of at most 0.012.
Values may be sent and summed in bfloat16 or wider, within the bound.
No kernel may reach another device: no remote copies, remote signals or barrier semaphores. Data moves between devices by JAX's collectives and lax.ppermute only.
A program may use at most 192 MiB of HBM per device.

```python
import math
import jax
import jax.numpy as jnp
from jax import lax

D = 5120
HEAD = 128
HEADS = 24
NT = 8
STEPS = 2
FTOK = 384
FRAMES = 16
TOKENS = 6144
N_DP = 8


def draw_tokens(key, part):
    frame_key, noise_key, scale_key = jax.random.split(key, 3)
    common = jax.random.normal(frame_key, (FRAMES, 1, D), jnp.float32)
    noise = jax.random.normal(noise_key, (FRAMES, FTOK, D), jnp.float32)
    row_scale = jnp.exp(jax.random.uniform(scale_key, (FRAMES, FTOK, 1), jnp.float32, 0.0, 0.7))
    values = (0.35 * common + 0.9 * noise) * row_scale
    return jnp.clip(values, -8.0, 8.0).reshape(TOKENS, D).astype(jnp.bfloat16)


def with_ends(values, key, least, top_value):
    extent = values.shape
    spot = [jax.random.randint(jax.random.fold_in(key, axis), (), 0, extent[axis]) for axis in range(len(extent))]
    values = values.at[tuple(spot)].set(least)
    longest = extent.index(max(extent))
    spot[longest] = (spot[longest] + 1) % extent[longest]
    return values.at[tuple(spot)].set(top_value)


def block_scale(rng, extent, pieces, least, top_value):
    def one(position, shards_of):
        heights = jax.random.uniform(jax.random.fold_in(jax.random.fold_in(rng, 6), position), (shards_of,), jnp.float32, least / len(pieces), top_value / len(pieces))
        return jnp.repeat(jnp.exp(heights), extent[position] // shards_of).reshape((-1,) + (1,) * (len(extent) - position - 1))

    loudness = one(*pieces[0])
    for cut in pieces[1:]:
        loudness = loudness * one(*cut)
    return loudness


def centred(key, extent, scale, reach, cuts=(), kind=jnp.bfloat16):
    array = jax.random.normal(key, extent, jnp.float32) * scale
    if len(cuts) > 0:
        array = block_scale(key, extent, cuts, -0.22, 0.18) * array
    return jnp.clip(array, min=-reach, max=reach).astype(kind)


def setup_inputs(seed: int = 0) -> dict:
    key_list = jax.random.split(jax.random.key(seed), 7)
    return {
        "tokens": draw_tokens(jax.random.fold_in(key_list[6], 71), 0),
        "qkv_weight": centred(key_list[1], (D, 3, HEADS * HEAD), D ** -0.5, 0.078125, ((2, 8),)),
        "out_weight": centred(key_list[2], (HEADS * HEAD, D), (HEADS * HEAD) ** -0.5, 0.109375, ((0, 8),)),
        "mod_table": centred(key_list[3], (NT, 3, D), 0.6, 3.0, (), jnp.float32),
        "levels": with_ends(jax.random.randint(key_list[4], (FRAMES,), 0, NT - STEPS + 1), jax.random.fold_in(key_list[4], 1), 0, NT - STEPS).astype(jnp.int32),
        "frame_order": jax.random.permutation(key_list[5], FRAMES).astype(jnp.int32),
    }


EPSILON = 1e-06

def layer_normed(values):
    average = lax.optimization_barrier(jnp.mean(values, axis=-1, keepdims=True))
    centered = values - average
    variance = lax.optimization_barrier(jnp.mean(centered * centered, axis=-1, keepdims=True))
    return centered * lax.rsqrt(variance + EPSILON)

def head_normed(values):
    return values * lax.rsqrt(lax.optimization_barrier(jnp.mean(values * values, axis=-1, keepdims=True)) + EPSILON)

def reference(tokens, qkv_weight, out_weight, mod_table, levels, frame_order):
    inner_width = HEADS * HEAD
    hidden = tokens.reshape(FRAMES, FTOK, D)
    weights_flat = qkv_weight.reshape(D, 3 * inner_width)
    key_frames = jnp.arange(TOKENS, dtype=jnp.int32) // FTOK
    key_ranks = frame_order[key_frames]
    factor = 1.0 / math.sqrt(HEAD)
    group_width = inner_width // N_DP
    attended = None
    for step_index in range(STEPS):
        chosen = mod_table[levels + step_index]
        shift_rows = chosen[:, 0][:, None, :]
        scale_rows = chosen[:, 1][:, None, :]
        gate_rows = chosen[:, 2][:, None, :]
        normed = (layer_normed(hidden.astype(jnp.float32)) * (1.0 + scale_rows) + shift_rows).astype(jnp.bfloat16)
        projected = jnp.dot(normed.reshape(TOKENS, D), weights_flat, preferred_element_type=jnp.float32)
        queries = head_normed(projected[:, :inner_width].reshape(TOKENS, HEADS, HEAD)).astype(jnp.bfloat16)
        key_rows = head_normed(projected[:, inner_width:2 * inner_width].reshape(TOKENS, HEADS, HEAD)).astype(jnp.bfloat16)
        value_rows = projected[:, 2 * inner_width:].reshape(TOKENS, HEADS, HEAD).astype(jnp.bfloat16)
        key_float = key_rows.astype(jnp.float32)
        value_float = value_rows.astype(jnp.float32)

        def one_frame(frame_query):
            query_block, query_rank = frame_query
            scores = jnp.einsum('qhd,khd->hqk', query_block.astype(jnp.float32), key_float) * factor
            weights = jnp.where((key_ranks <= query_rank)[None, None, :], jnp.exp(scores), 0.0)
            row_total = lax.optimization_barrier(jnp.sum(weights, axis=-1))
            mixture = jnp.einsum('hqk,khd->qhd', weights.astype(jnp.bfloat16).astype(jnp.float32), value_float)
            return (mixture / jnp.transpose(row_total)[:, :, None]).astype(jnp.bfloat16)
        attended = lax.map(one_frame, (queries.reshape(FRAMES, FTOK, HEADS, HEAD), frame_order))
        attended = attended.reshape(TOKENS, inner_width)
        branch = jnp.zeros((TOKENS, D), jnp.float32)
        for group_index in range(N_DP):
            low = group_index * group_width
            partial_term = jnp.dot(attended[:, low:low + group_width], out_weight[low:low + group_width], preferred_element_type=jnp.float32)
            rounded = lax.optimization_barrier(partial_term.astype(jnp.bfloat16))
            branch = branch + rounded.astype(jnp.float32)
        hidden = (hidden.astype(jnp.float32) + gate_rows * branch.reshape(FRAMES, FTOK, D)).astype(jnp.bfloat16)
    return (hidden.reshape(TOKENS, D), attended)
```

```python
import math

import jax
import jax.numpy as jnp
from jax import lax
from jax.experimental import pallas as pl
from jax.experimental.pallas import tpu as pltpu
from jax.sharding import PartitionSpec as P

HEAD = 128
STEPS = 2
EPSILON = 1e-06
ROWS = 16
VMEM = 56 * 1024 * 1024
GROUP = 8
FRAMES = 16


def over_dp(value, to):
    return lax.ppermute(value, "dp", [(d, to(d) % GROUP) for d in range(GROUP)])


def over_frame(value, to):
    return lax.ppermute(value, "frame", [(f, to(f) % FRAMES) for f in range(FRAMES)])


def gathered(block):
    beside = over_dp(block, lambda d: d ^ 1)
    below = over_dp(block, lambda d: d + 2)
    above = over_dp(block, lambda d: d - 2)
    across = over_dp(block, lambda d: d + 4)
    beside_below = over_dp(beside, lambda d: d + 2)
    beside_above = over_dp(beside, lambda d: d - 2)
    beside_across = over_dp(across, lambda d: d ^ 1)
    return [block, beside, below, above, across, beside_below, beside_above, beside_across]


def origins(d):
    other = d ^ 1
    return [
        d,
        other,
        (d + 6) % GROUP,
        (d + 2) % GROUP,
        (d + 4) % GROUP,
        (other + 6) % GROUP,
        (other + 2) % GROUP,
        (other + 4) % GROUP,
    ]


def normed_rows(x, scale, shift):
    centered = x - jnp.mean(x, axis=-1, keepdims=True)
    variance = jnp.mean(centered * centered, axis=-1, keepdims=True)
    return (centered * lax.rsqrt(variance + EPSILON) * (1.0 + scale) + shift).astype(jnp.bfloat16)


def project(normed, w_ref, q_ref, kv_ref):
    turn = pl.program_id(0)
    product = jnp.dot(normed[...], w_ref[0], preferred_element_type=jnp.float32)

    def head_normed(block):
        return block * lax.rsqrt(jnp.mean(block * block, axis=-1, keepdims=True) + EPSILON)

    heads = [slice(low, low + HEAD) for low in range(0, product.shape[1], HEAD)]

    @pl.when(turn == 0)
    def _():
        for cut in heads:
            kv_ref[0, :, cut] = head_normed(product[:, cut]).astype(jnp.bfloat16)

    @pl.when(turn == 1)
    def _():
        kv_ref[0] = product.astype(jnp.bfloat16)

    @pl.when(turn == 2)
    def _():
        for cut in heads:
            q_ref[:, cut] = head_normed(product[:, cut]).astype(jnp.bfloat16)


def qkv_from_rows(info, *refs):
    blocks, (mod_ref, w_ref, q_ref, kv_ref, own_ref, normed) = refs[:GROUP], refs[GROUP:]
    own_rows = blocks[0].shape[0]
    width = own_ref.shape[1]

    @pl.when(pl.program_id(0) == 0)
    def _():
        columns = pl.ds(pl.multiple_of(info[1] * width, HEAD), width)
        for index, block in enumerate(blocks):
            first = info[1 + index] * own_rows
            own_ref[pl.ds(pl.multiple_of(first, ROWS), own_rows), :] = block[:, columns]

            def one(step, carry, block=block, first=first):
                low = pl.multiple_of(step * ROWS, ROWS)
                x = block[pl.ds(low, ROWS), :].astype(jnp.float32)
                normed[pl.ds(pl.multiple_of(first + low, ROWS), ROWS), :] = normed_rows(
                    x, mod_ref[0, 1:2, :], mod_ref[0, 0:1, :]
                )
                return carry

            lax.fori_loop(0, own_rows // ROWS, one, 0)

    project(normed, w_ref, q_ref, kv_ref)


def qkv_from_columns(info, *refs):
    blocks, (mod_ref, w_ref, q_ref, kv_ref, normed) = refs[:GROUP], refs[GROUP:]
    rows, width = blocks[0].shape
    total = width * GROUP

    @pl.when(pl.program_id(0) == 0)
    def _():
        places = [
            pl.ds(pl.multiple_of(info[1 + index] * width, HEAD), width) for index in range(GROUP)
        ]

        def one(step, carry):
            band = pl.ds(pl.multiple_of(step * ROWS, ROWS), ROWS)
            parts = [block[band, :].astype(jnp.float32) for block in blocks]
            mean = sum(jnp.sum(part, axis=-1, keepdims=True) for part in parts) / total
            parts = [part - mean for part in parts]
            variance = (
                sum(jnp.sum(part * part, axis=-1, keepdims=True) for part in parts) / total
            )
            factor = lax.rsqrt(variance + EPSILON)
            for part, place in zip(parts, places):
                normed[band, place] = (
                    part * factor * (1.0 + mod_ref[0, 1:2, place]) + mod_ref[0, 0:1, place]
                ).astype(jnp.bfloat16)
            return carry

        lax.fori_loop(0, rows // ROWS, one, 0)

    project(normed, w_ref, q_ref, kv_ref)


def qkv(blocks, by_rows, info, mod_table, weights):
    width, inner = weights.shape[1:]
    rows = blocks[0].shape[0] * (GROUP if by_rows else 1)
    whole = lambda shape: pl.BlockSpec(shape, lambda j, info: (0,) * len(shape))
    out_shape = [
        jax.ShapeDtypeStruct((rows, inner), jnp.bfloat16),
        jax.ShapeDtypeStruct((2, rows, inner), jnp.bfloat16),
    ]
    out_specs = [
        whole((rows, inner)),
        pl.BlockSpec((1, rows, inner), lambda j, info: (jnp.minimum(j, 1), 0, 0)),
    ]
    if by_rows:
        out_shape.append(jax.ShapeDtypeStruct((rows, width // GROUP), jnp.bfloat16))
        out_specs.append(whole((rows, width // GROUP)))
    return pl.pallas_call(
        qkv_from_rows if by_rows else qkv_from_columns,
        out_shape=out_shape,
        grid_spec=pltpu.PrefetchScalarGridSpec(
            num_scalar_prefetch=1,
            grid=(3,),
            in_specs=[whole(block.shape) for block in blocks]
            + [
                pl.BlockSpec((1, 3, width), lambda j, info: (info[0], 0, 0)),
                pl.BlockSpec((1, width, inner), lambda j, info: ((j + 1) % 3, 0, 0)),
            ],
            out_specs=out_specs,
            scratch_shapes=[pltpu.VMEM((rows, width), jnp.bfloat16)],
        ),
        compiler_params=pltpu.CompilerParams(vmem_limit_bytes=VMEM),
        cost_estimate=pl.CostEstimate(
            flops=6 * rows * width * inner,
            bytes_accessed=6 * width * inner + 2 * rows * width,
            transcendentals=0,
        ),
        name="qkv",
    )(info, *blocks, mod_table, weights)


def attend_kernel(info, qa_ref, qb_ref, *refs):
    kv = [(refs[2 * i], refs[2 * i + 1]) for i in range(4)]
    keep_ref, keep_sum_ref, send_ref, acc = refs[8:]
    head, half = pl.program_id(0), pl.program_id(1)
    rows = qa_ref.shape[0]
    inner = keep_ref.shape[1]
    factor = math.log2(math.e) / math.sqrt(HEAD)
    band = pl.ds(pl.multiple_of(half * rows, ROWS), rows)
    place = pl.ds(pl.multiple_of(head * HEAD, HEAD), HEAD)
    lanes = lax.broadcasted_iota(jnp.int32, (rows, HEAD), 1)
    for side, q_ref in enumerate((qa_ref, qb_ref)):
        acc[...] = jnp.zeros_like(acc)
        rank = info[side * 2 + half]
        for index, (k_ref, v_ref) in enumerate(kv):

            @pl.when(info[4 + index] <= rank)
            def _(q_ref=q_ref, k_ref=k_ref, v_ref=v_ref):
                scores = lax.dot_general(
                    q_ref[...],
                    k_ref[0],
                    (((1,), (1,)), ((), ())),
                    preferred_element_type=jnp.float32,
                )
                weights = jnp.exp2(scores * factor).astype(jnp.bfloat16)
                values = v_ref[0]
                acc[...] += jnp.dot(
                    weights,
                    jnp.concatenate([values, jnp.ones_like(values)], axis=1),
                    preferred_element_type=jnp.float32,
                )

        total = acc[:, HEAD:]
        if side == 0:
            keep_ref[band, place] = acc[:, :HEAD]

            @pl.when(head == 0)
            def _():
                keep_sum_ref[band, :] = jnp.where(lanes == 0, total, 0.0)

            @pl.when(head > 0)
            def _():
                keep_sum_ref[band, :] = jnp.where(lanes == head, total, keep_sum_ref[band, :])
        else:
            send_ref[band, place] = acc[:, :HEAD].astype(jnp.bfloat16)
            coarse = total.astype(jnp.bfloat16)
            fine = (total - coarse.astype(jnp.float32)).astype(jnp.bfloat16)
            pair = jnp.where(
                lanes == head,
                coarse.astype(jnp.float32),
                jnp.where(lanes == head + 3, fine.astype(jnp.float32), 0.0),
            )

            @pl.when(head == 0)
            def _():
                send_ref[band, inner:] = pair.astype(jnp.bfloat16)

            @pl.when(head > 0)
            def _():
                send_ref[band, inner:] = (
                    pair + send_ref[band, inner:].astype(jnp.float32)
                ).astype(jnp.bfloat16)


def attend(qa, qb, kvs, info):
    rows = qa.shape[0] // 2
    inner = qa.shape[1]
    whole = lambda shape: pl.BlockSpec(shape, lambda h, i, info: (0,) * len(shape))
    specs, operands = [], []
    for kv in kvs:
        for which in range(2):
            specs.append(
                pl.BlockSpec((1, rows, HEAD), lambda h, i, info, which=which: (which, 0, h))
            )
            operands.append(kv)
    return pl.pallas_call(
        attend_kernel,
        out_shape=[
            jax.ShapeDtypeStruct((2 * rows, inner), jnp.float32),
            jax.ShapeDtypeStruct((2 * rows, HEAD), jnp.float32),
            jax.ShapeDtypeStruct((2 * rows, inner + HEAD), jnp.bfloat16),
        ],
        grid_spec=pltpu.PrefetchScalarGridSpec(
            num_scalar_prefetch=1,
            grid=(inner // HEAD, 2),
            in_specs=[pl.BlockSpec((rows, HEAD), lambda h, i, info: (i, h))] * 2 + specs,
            out_specs=[
                whole((2 * rows, inner)),
                whole((2 * rows, HEAD)),
                whole((2 * rows, inner + HEAD)),
            ],
            scratch_shapes=[pltpu.VMEM((rows, 2 * HEAD), jnp.float32)],
        ),
        compiler_params=pltpu.CompilerParams(vmem_limit_bytes=VMEM),
        cost_estimate=pl.CostEstimate(
            flops=64 * rows * rows * inner,
            bytes_accessed=32 * rows * inner,
            transcendentals=16 * rows * rows * 3,
        ),
        name="attend",
    )(info, qa, qb, *operands)


def received_sums(ref, inner):
    pair = ref[:, inner:].astype(jnp.float32)
    return pair + pltpu.roll(pair, HEAD - 3, 1)


def over_cores_kernel(keep_ref, keep_sum_ref, got_ref, own_ref, own_sum_ref, send_ref):
    rows, inner = own_ref.shape
    own, other = slice(0, rows), slice(rows, 2 * rows)
    sums = keep_sum_ref[...] + received_sums(got_ref, inner)
    own_ref[...] = keep_ref[own, :] + got_ref[own, :inner].astype(jnp.float32)
    own_sum_ref[...] = sums[own, :]
    send_ref[:, :inner] = (
        keep_ref[other, :] + got_ref[other, :inner].astype(jnp.float32)
    ).astype(jnp.bfloat16)
    lanes = lax.broadcasted_iota(jnp.int32, (rows, HEAD), 1)
    theirs = sums[other, :]
    coarse = theirs.astype(jnp.bfloat16).astype(jnp.float32)
    send_ref[:, inner:] = jnp.where(
        lanes < 3, coarse, pltpu.roll(theirs - coarse, 3, 1)
    ).astype(jnp.bfloat16)


def over_cores(keep, keep_sum, got):
    rows, inner = keep.shape[0] // 2, keep.shape[1]
    return pl.pallas_call(
        over_cores_kernel,
        out_shape=[
            jax.ShapeDtypeStruct((rows, inner), jnp.float32),
            jax.ShapeDtypeStruct((rows, HEAD), jnp.float32),
            jax.ShapeDtypeStruct((rows, inner + HEAD), jnp.bfloat16),
        ],
        compiler_params=pltpu.CompilerParams(vmem_limit_bytes=VMEM),
        name="over_cores",
    )(keep, keep_sum, got)


def finish_kernel(own_ref, own_sum_ref, got_ref, out_ref):
    inner = own_ref.shape[1]
    sums = own_sum_ref[...] + received_sums(got_ref, inner)
    for head in range(inner // HEAD):
        cut = slice(head * HEAD, (head + 1) * HEAD)
        out_ref[:, cut] = (
            (own_ref[:, cut] + got_ref[:, cut].astype(jnp.float32)) / sums[:, head : head + 1]
        ).astype(jnp.bfloat16)


def finish(own, own_sum, got):
    return pl.pallas_call(
        finish_kernel,
        out_shape=jax.ShapeDtypeStruct(own.shape, jnp.bfloat16),
        compiler_params=pltpu.CompilerParams(vmem_limit_bytes=VMEM),
        name="finish",
    )(own, own_sum, got)


def branch_kernel(info, *refs):
    parts, (w_ref, hidden_ref, mod_ref, out_ref) = refs[:GROUP], refs[GROUP:]
    width = hidden_ref.shape[1]
    total = None
    for index, part in enumerate(parts):
        term = jnp.dot(part[...], w_ref[info[1 + index]], preferred_element_type=jnp.float32)
        total = term if total is None else total + term
    columns = pl.ds(pl.multiple_of(info[1] * width, HEAD), width)
    out_ref[...] = (hidden_ref[...].astype(jnp.float32) + mod_ref[0, 2:3, columns] * total).astype(
        jnp.bfloat16
    )


def add_branch(parts, weights, hidden, mod_table, info):
    whole = lambda shape: pl.BlockSpec(shape, lambda j, info: (0,) * len(shape))
    full = mod_table.shape[2]
    return pl.pallas_call(
        branch_kernel,
        out_shape=jax.ShapeDtypeStruct(hidden.shape, jnp.bfloat16),
        grid_spec=pltpu.PrefetchScalarGridSpec(
            num_scalar_prefetch=1,
            grid=(1,),
            in_specs=[whole(part.shape) for part in parts]
            + [
                whole(weights.shape),
                whole(hidden.shape),
                pl.BlockSpec((1, 3, full), lambda j, info: (info[0], 0, 0)),
            ],
            out_specs=whole(hidden.shape),
        ),
        compiler_params=pltpu.CompilerParams(vmem_limit_bytes=VMEM),
        name="add_branch",
    )(info, *parts, weights, hidden, mod_table)


def out_columns(out_weight, core, after):
    rows, width = out_weight.shape
    half = rows // 2
    own = lax.dynamic_slice(out_weight, (core * half, 0), (half, width))
    own = jnp.transpose(own.reshape(half, GROUP, width // GROUP), (1, 0, 2))
    own, after = lax.optimization_barrier((own, after))
    mine = lax.all_to_all(own, "dp", 0, 0, tiled=True)
    theirs = over_frame(mine, lambda f: f ^ 1)
    first = core == 0
    return jnp.concatenate(
        [jnp.where(first, mine, theirs), jnp.where(first, theirs, mine)], axis=1
    )


def per_device(tokens, qkv_weight, out_weight, mod_table, levels, frame_order):
    own_rows, width = tokens.shape
    frame = lax.axis_index("frame")
    place = lax.axis_index("dp")
    level = levels[frame]
    where = origins(place)
    rank = lambda f: frame_order[f % FRAMES]
    ranks = jnp.stack(
        [
            rank(frame),
            rank(frame ^ 2),
            rank(frame ^ 1),
            rank(frame ^ 3),
            rank(frame),
            rank(frame + 12),
            rank(frame + 4),
            rank(frame + 8),
        ]
    ).astype(jnp.int32)
    blocks = gathered(tokens)
    weights = jnp.transpose(qkv_weight, (1, 0, 2))
    own_hidden = None
    out_weights = None
    attended = None
    for step_index in range(STEPS):
        info = jnp.stack([level + step_index] + where).astype(jnp.int32)
        if step_index == 0:
            q, kv, own_hidden = qkv(blocks, True, info, mod_table, weights)
        else:
            q, kv = qkv(blocks, False, info, mod_table, weights)
        kvs = [
            kv,
            over_frame(kv, lambda f: f + 4),
            over_frame(kv, lambda f: f - 4),
            over_frame(kv, lambda f: f + 8),
        ]
        qa = jnp.concatenate([q, over_frame(q, lambda f: f ^ 2)], axis=0)
        qb = over_frame(qa, lambda f: f ^ 1)
        if step_index == 0:
            out_weights = out_columns(out_weight, frame % 2, kv)
        keep, keep_sum, send = attend(qa, qb, kvs, ranks)
        own, own_sum, send = over_cores(keep, keep_sum, over_frame(send, lambda f: f ^ 1))
        attended = finish(own, own_sum, over_frame(send, lambda f: f ^ 2))
        own_hidden = add_branch(gathered(attended), out_weights, own_hidden, mod_table, info)
        if step_index < STEPS - 1:
            blocks = gathered(own_hidden)
    pieces = own_hidden.reshape(GROUP, own_rows, width // GROUP)
    pieces = lax.all_to_all(pieces, "dp", 0, 0, tiled=True)
    hidden = jnp.transpose(pieces, (1, 0, 2)).reshape(own_rows, width)
    return (hidden, attended)


def solution(mesh):
    return jax.shard_map(
        per_device,
        mesh=mesh,
        in_specs=(P(("frame", "dp"), None), P(None, None, "dp"), P("dp", None), P(), P(), P()),
        out_specs=(P(("frame", "dp"), None), P("frame", "dp")),
        check_vma=False,
    )
```

```python
import math

import jax
import jax.numpy as jnp
import numpy as np
from jax import lax
from jax.experimental import pallas as pl
from jax.experimental.pallas import tpu as pltpu
from jax.sharding import PartitionSpec as P

HEAD = 128
STEPS = 2
EPSILON = 1e-06
ROWS = 16
GROUP = 8
FRAMES = 16


def over_dp(value, to):
    return lax.ppermute(value, "dp", [(d, to(d) % GROUP) for d in range(GROUP)])


def over_frame(value, to):
    return lax.ppermute(value, "frame", [(f, to(f) % FRAMES) for f in range(FRAMES)])


def gathered(block):
    beside = over_dp(block, lambda d: d ^ 1)
    below = over_dp(block, lambda d: d + 2)
    above = over_dp(block, lambda d: d - 2)
    across = over_dp(block, lambda d: d + 4)
    beside_below = over_dp(beside, lambda d: d + 2)
    beside_above = over_dp(beside, lambda d: d - 2)
    beside_across = over_dp(across, lambda d: d ^ 1)
    return [block, beside, below, above, across, beside_below, beside_above, beside_across]


def origins(d):
    swap = np.array([0, 1, 0, 0, 0, 1, 1, 1], np.int32)
    shift = np.array([0, 0, 6, 2, 4, 6, 2, 4], np.int32)
    return ((d ^ swap) + shift) % GROUP


CHUNKS = 4


def local_call(kernel, name, info, operands, outs, scratch=(), limit=16, flops=0, moved=0):
    placed = [pltpu.with_memory_space_constraint(value, pltpu.VMEM) for value in operands]
    in_vmem = pl.BlockSpec(memory_space=pltpu.VMEM)
    return pl.pallas_call(
        kernel,
        out_shape=[pltpu.VMEM(shape, kind) for shape, kind in outs],
        in_specs=[pl.BlockSpec(memory_space=pltpu.SMEM)] + [in_vmem] * len(operands),
        out_specs=[in_vmem] * len(outs),
        scratch_shapes=list(scratch),
        compiler_params=pltpu.CompilerParams(vmem_limit_bytes=limit * 1024 * 1024),
        cost_estimate=pl.CostEstimate(flops=flops, bytes_accessed=moved, transcendentals=0),
        name=name,
    )(info, *placed)


def load_kernel(info, source, target, sems):
    del info
    copies = []
    for part in range(GROUP):
        span = source.shape[1] // GROUP
        cut = pl.ds(part * span, span)
        copies.append(
            pltpu.make_async_copy(source.at[:, cut, :], target.at[:, cut, :], sems.at[part])
        )
        copies[-1].start()
    for copy in copies:
        copy.wait()


def load(weights, info):
    return pl.pallas_call(
        load_kernel,
        out_shape=pltpu.VMEM(weights.shape, weights.dtype),
        in_specs=[pl.BlockSpec(memory_space=pltpu.SMEM), pl.BlockSpec(memory_space=pl.ANY)],
        out_specs=pl.BlockSpec(memory_space=pltpu.VMEM),
        scratch_shapes=[pltpu.SemaphoreType.DMA((GROUP,))],
        compiler_params=pltpu.CompilerParams(vmem_limit_bytes=2 * 1024 * 1024),
        cost_estimate=pl.CostEstimate(flops=0, bytes_accessed=2 * weights.size, transcendentals=0),
        name="load",
    )(info, weights)


EARLY = 5


def folded(values):
    return sum(values[:, low : low + HEAD] for low in range(0, values.shape[1], HEAD))


def moments(parts, pivot):
    shifted = [part - pivot for part in parts]
    return folded(sum(shifted)), folded(sum(part * part for part in shifted))


def keep_moments(mean_ref, factor_ref, band, pivot, first, second, full):
    first = jnp.sum(first, axis=-1, keepdims=True) / full
    second = jnp.sum(second, axis=-1, keepdims=True) / full
    variance = second - first * first
    mean_ref[band, :] = jnp.broadcast_to(pivot + first, (ROWS, HEAD))
    factor_ref[band, :] = jnp.broadcast_to(lax.rsqrt(variance + EPSILON), (ROWS, HEAD))


def normed(values, mean, factor, mod_ref, place):
    centered = values.astype(jnp.float32) - mean
    return (centered * factor * (1.0 + mod_ref[1:2, place]) + mod_ref[0:1, place]).astype(
        jnp.bfloat16
    )


def products(norm, chunks, weight):
    norm(0)
    totals = [None] * 3
    for chunk in range(CHUNKS):
        if chunk + 1 < CHUNKS:
            norm(chunk + 1)
        for which in range(3):
            term = jnp.dot(
                chunks[chunk][...], weight(which, chunk), preferred_element_type=jnp.float32
            )
            totals[which] = term if chunk == 0 else totals[which] + term
    return totals


def head_normed(values):
    blocks = []
    for low in range(0, values.shape[1], HEAD):
        block = values[:, low : low + HEAD]
        blocks.append(
            block * lax.rsqrt(jnp.mean(block * block, axis=-1, keepdims=True) + EPSILON)
        )
    return jnp.concatenate(blocks, axis=1).astype(jnp.bfloat16)


def rows_projected(blocks, mod_ref, w_ref, mean_ref, factor_ref, chunks):
    own_rows, full = blocks[0].shape
    width = full // GROUP
    span = full // CHUNKS
    for index, block in enumerate(blocks):

        def one(step, carry, index=index, block=block):
            low = pl.multiple_of(step * ROWS, ROWS)
            band = block[pl.ds(low, ROWS), :].astype(jnp.float32)
            parts = [band[:, chunk * width : (chunk + 1) * width] for chunk in range(GROUP)]
            pivot = jnp.mean(parts[0], axis=-1, keepdims=True)
            keep_moments(
                mean_ref,
                factor_ref,
                pl.ds(pl.multiple_of(index * own_rows + low, ROWS), ROWS),
                pivot,
                *moments(parts, pivot),
                full,
            )
            return carry

        lax.fori_loop(0, own_rows // ROWS, one, 0)

    def norm(chunk):
        cut = slice(chunk * span, (chunk + 1) * span)
        for index, block in enumerate(blocks):
            band = slice(index * own_rows, (index + 1) * own_rows)
            chunks[chunk][band, :] = normed(
                block[:, cut], mean_ref[band, :1], factor_ref[band, :1], mod_ref, cut
            )

    totals = products(
        norm, chunks, lambda which, chunk: w_ref[which, chunk * span : (chunk + 1) * span, :]
    )
    return head_normed(totals[0]), head_normed(totals[1]), totals[2].astype(jnp.bfloat16)


def rows_early_kernel(info, *refs):
    del info
    blocks, (mod_ref, w_ref, out_ref, mean_ref, factor_ref) = refs[:EARLY], refs[EARLY:-CHUNKS]
    found = rows_projected(blocks, mod_ref, w_ref, mean_ref, factor_ref, refs[-CHUNKS:])
    for which in range(3):
        out_ref[which] = found[which]


def rows_late_kernel(info, *refs):
    blocks, rest = refs[:GROUP], refs[GROUP:-CHUNKS]
    mod_ref, w_ref, early_ref, q_ref, kv_ref, own_ref, mean_ref, factor_ref = rest
    found = rows_projected(blocks[EARLY:], mod_ref, w_ref, mean_ref, factor_ref, refs[-CHUNKS:])
    own_rows = blocks[0].shape[0]
    width = own_ref.shape[1]
    columns = pl.ds(pl.multiple_of(info[0] * width, HEAD), width)
    for index, block in enumerate(blocks):
        place = pl.ds(pl.multiple_of(info[index] * own_rows, ROWS), own_rows)
        own_ref[place, :] = block[:, columns]
        if index < EARLY:
            band = slice(index * own_rows, (index + 1) * own_rows)
            q_ref[place, :] = early_ref[0, band, :]
            kv_ref[0, place, :] = early_ref[1, band, :]
            kv_ref[1, place, :] = early_ref[2, band, :]
        else:
            band = slice((index - EARLY) * own_rows, (index - EARLY + 1) * own_rows)
            q_ref[place, :] = found[0][band]
            kv_ref[0, place, :] = found[1][band]
            kv_ref[1, place, :] = found[2][band]


def project_rows(blocks, info, mod_rows, weights):
    full, inner = weights.shape[1:]
    own_rows = blocks[0].shape[0]
    rows = own_rows * GROUP
    scratch = lambda count: (
        [pltpu.VMEM((count * own_rows, HEAD), jnp.float32)] * 2
        + [pltpu.VMEM((count * own_rows, full // CHUNKS), jnp.bfloat16)] * CHUNKS
    )
    early = local_call(
        rows_early_kernel,
        "rows_early",
        info,
        [*blocks[:EARLY], mod_rows, weights],
        [((3, EARLY * own_rows, inner), jnp.bfloat16)],
        scratch(EARLY),
        flops=6 * EARLY * own_rows * full * inner,
        moved=6 * full * inner,
    )[0]
    return local_call(
        rows_late_kernel,
        "rows_late",
        info,
        [*blocks, mod_rows, weights, early],
        [
            ((rows, inner), jnp.bfloat16),
            ((2, rows, inner), jnp.bfloat16),
            ((rows, full // GROUP), jnp.bfloat16),
        ],
        scratch(GROUP - EARLY),
        flops=6 * (GROUP - EARLY) * own_rows * full * inner,
        moved=6 * full * inner,
    )


def moments_kernel(info, *refs):
    del info
    blocks, out_ref = refs[:EARLY], refs[EARLY]
    rows = blocks[0].shape[0]

    def one(step, carry):
        band = pl.ds(pl.multiple_of(step * ROWS, ROWS), ROWS)
        parts = [block[band, :].astype(jnp.float32) for block in blocks]
        pivot = jnp.mean(parts[0], axis=-1, keepdims=True)
        out_ref[0, band, :] = jnp.broadcast_to(pivot, (ROWS, HEAD))
        out_ref[1, band, :], out_ref[2, band, :] = moments(parts, pivot)
        return carry

    lax.fori_loop(0, rows // ROWS, one, 0)


def columns_kernel(info, *refs):
    blocks, rest, chunks = refs[:GROUP], refs[GROUP:-CHUNKS], refs[-CHUNKS:]
    mod_ref, w_ref, early_ref, q_ref, kv_ref, mean_ref, factor_ref = rest
    rows, width = blocks[0].shape
    full = width * GROUP
    each = GROUP // CHUNKS

    def one(step, carry):
        band = pl.ds(pl.multiple_of(step * ROWS, ROWS), ROWS)
        pivot = early_ref[0, band, :1]
        first, second = moments(
            [block[band, :].astype(jnp.float32) for block in blocks[EARLY:]], pivot
        )
        keep_moments(
            mean_ref,
            factor_ref,
            band,
            pivot,
            first + early_ref[1, band, :],
            second + early_ref[2, band, :],
            full,
        )
        return carry

    lax.fori_loop(0, rows // ROWS, one, 0)
    place = lambda index: pl.ds(pl.multiple_of(info[index] * width, HEAD), width)

    def norm(chunk):
        for part in range(each):
            index = chunk * each + part
            chunks[chunk][:, part * width : (part + 1) * width] = normed(
                blocks[index][...], mean_ref[:, :1], factor_ref[:, :1], mod_ref, place(index)
            )

    def weight(which, chunk):
        return jnp.concatenate(
            [w_ref[which, place(chunk * each + part), :] for part in range(each)], axis=0
        )

    totals = products(norm, chunks, weight)
    q_ref[...] = head_normed(totals[0])
    kv_ref[0] = head_normed(totals[1])
    kv_ref[1] = totals[2].astype(jnp.bfloat16)


def project_columns(blocks, info, mod_rows, weights):
    full, inner = weights.shape[1:]
    rows = blocks[0].shape[0]
    early = local_call(
        moments_kernel,
        "moments",
        info,
        blocks[:EARLY],
        [((3, rows, HEAD), jnp.float32)],
        flops=rows * full,
        moved=2 * EARLY * blocks[0].size,
    )[0]
    return local_call(
        columns_kernel,
        "columns",
        info,
        [*blocks, mod_rows, weights, early],
        [((rows, inner), jnp.bfloat16), ((2, rows, inner), jnp.bfloat16)],
        [pltpu.VMEM((rows, HEAD), jnp.float32)] * 2
        + [pltpu.VMEM((rows, full // CHUNKS), jnp.bfloat16)] * CHUNKS,
        flops=6 * rows * full * inner,
        moved=6 * full * inner,
    )


def attend_kernel(info, *refs):
    queries, kvs = refs[:4], refs[4:8]
    own_ref, own_sum_ref, sends = refs[8], refs[9], refs[10:13]
    q_all, kv_all, total = refs[13:]
    rows, inner = own_ref.shape
    heads = inner // HEAD
    factor = math.log2(math.e) / math.sqrt(HEAD)
    for index in range(4):
        q_all[index] = queries[index][...]
        kv_all[index] = kvs[index][...]
    total[...] = jnp.zeros_like(total)

    def one(step, carry):
        mine, theirs = step // 4, step % 4

        @pl.when(info[4 + theirs] <= info[mine])
        def _():
            weights = []
            for head in range(heads):
                cut = slice(head * HEAD, (head + 1) * HEAD)
                scores = lax.dot_general(
                    q_all[mine, :, cut],
                    kv_all[theirs, 0, :, cut],
                    (((1,), (1,)), ((), ())),
                    preferred_element_type=jnp.float32,
                )
                weights.append(jnp.exp2(scores * factor).astype(jnp.bfloat16))
            for head in range(heads):
                values = kv_all[theirs, 1, :, head * HEAD : (head + 1) * HEAD]
                total[mine, head] += jnp.dot(
                    weights[head],
                    jnp.concatenate([values, jnp.ones_like(values)], axis=1),
                    preferred_element_type=jnp.float32,
                )

        return carry

    lax.fori_loop(0, 16, one, 0)
    lanes = lax.broadcasted_iota(jnp.int32, (rows, HEAD), 1)
    for index in range(4):
        sums = jnp.zeros((rows, HEAD), jnp.float32)
        for head in range(heads):
            cut = slice(head * HEAD, (head + 1) * HEAD)
            numerator, row_total = total[index, head, :, :HEAD], total[index, head, :, HEAD:]
            if index == 0:
                own_ref[:, cut] = numerator
                sums = jnp.where(lanes == head, row_total, sums)
            else:
                sends[index - 1][:rows, cut] = numerator.astype(jnp.bfloat16)
                coarse = row_total.astype(jnp.bfloat16).astype(jnp.float32)
                sums = jnp.where(lanes == head, coarse, sums)
                sums = jnp.where(lanes == heads + head, row_total - coarse, sums)
        if index == 0:
            own_sum_ref[...] = sums
        else:
            sends[index - 1][rows:, :] = sums.T[:ROWS].astype(jnp.bfloat16)


def attend(queries, kvs, info):
    rows, inner = queries[0].shape
    heads = inner // HEAD
    return local_call(
        attend_kernel,
        "attend",
        info,
        [*queries, *kvs],
        [((rows, inner), jnp.float32), ((rows, HEAD), jnp.float32)]
        + [((rows + ROWS, inner), jnp.bfloat16)] * 3,
        [
            pltpu.VMEM((4, rows, inner), jnp.bfloat16),
            pltpu.VMEM((4, 2, rows, inner), jnp.bfloat16),
            pltpu.VMEM((4, heads, rows, 2 * HEAD), jnp.float32),
        ],
        limit=24,
        flops=64 * rows * rows * inner,
        moved=32 * rows * inner,
    )


def finish_kernel(info, own_ref, own_sum_ref, *refs):
    del info
    got, out_ref = refs[:3], refs[3]
    rows, inner = own_ref.shape
    heads = inner // HEAD
    pairs = sum(ref[rows:, :].astype(jnp.float32) for ref in got)
    pairs = jnp.concatenate([pairs, jnp.zeros((HEAD - ROWS, inner), jnp.float32)], axis=0).T
    for head in range(heads):
        cut = slice(head * HEAD, (head + 1) * HEAD)
        row_total = (
            own_sum_ref[:, head : head + 1]
            + pairs[:, head : head + 1]
            + pairs[:, heads + head : heads + head + 1]
        )
        numerator = own_ref[:, cut] + sum(ref[:rows, cut].astype(jnp.float32) for ref in got)
        out_ref[:, cut] = (numerator / row_total).astype(jnp.bfloat16)


def finish(own, own_sum, got, info):
    return local_call(
        finish_kernel,
        "finish",
        info,
        [own, own_sum, *got],
        [(own.shape, jnp.bfloat16)],
    )[0]


def early_kernel(info, *refs):
    parts, (w_ref, out_ref) = refs[:EARLY], refs[EARLY:]
    out_ref[...] = sum(
        jnp.dot(part[...], w_ref[info[index]], preferred_element_type=jnp.float32)
        for index, part in enumerate(parts)
    )


def late_kernel(info, *refs):
    count = GROUP - EARLY
    parts, (sum_ref, w_ref, hidden_ref, mod_ref, out_ref) = refs[:count], refs[count:]
    width = hidden_ref.shape[1]
    total = sum_ref[...] + sum(
        jnp.dot(part[...], w_ref[info[EARLY + index]], preferred_element_type=jnp.float32)
        for index, part in enumerate(parts)
    )
    columns = pl.ds(pl.multiple_of(info[0] * width, HEAD), width)
    out_ref[...] = (hidden_ref[...].astype(jnp.float32) + mod_ref[2:3, columns] * total).astype(
        jnp.bfloat16
    )


def add_branch(parts, weights, hidden, mod_rows, info):
    rows, inner = parts[0].shape
    each = 2 * rows * inner * hidden.shape[1]
    moved = 4 * hidden.size
    early = local_call(
        early_kernel,
        "early",
        info,
        [*parts[:EARLY], weights],
        [(hidden.shape, jnp.float32)],
        flops=EARLY * each,
        moved=moved,
    )[0]
    return local_call(
        late_kernel,
        "late",
        info,
        [*parts[EARLY:], early, weights, hidden, mod_rows],
        [(hidden.shape, jnp.bfloat16)],
        flops=(GROUP - EARLY) * each,
        moved=moved,
    )[0]


def out_pieces(out_weight, core):
    rows, width = out_weight.shape
    half = rows // 2
    own = lax.dynamic_slice(out_weight, (core * half, 0), (half, width))
    return jnp.transpose(own.reshape(half, GROUP, width // GROUP), (1, 0, 2))


def out_columns(mine, core):
    theirs = over_frame(mine, lambda f: f ^ 1)
    first = core == 0
    return jnp.concatenate(
        [jnp.where(first, mine, theirs), jnp.where(first, theirs, mine)], axis=1
    )


def per_device(tokens, qkv_weight, out_weight, mod_table, levels, frame_order):
    own_rows, width = tokens.shape
    frame = lax.axis_index("frame")
    ids = jnp.arange(FRAMES, dtype=jnp.int32)
    level = jnp.sum(jnp.where(ids == frame, levels, 0))
    where = origins(lax.axis_index("dp")).astype(jnp.int32)
    shift = np.array([0, 12, 4, 8, 0, 0, 0, 0], np.int32)
    swap = np.array([0, 0, 0, 0, 0, 2, 1, 3], np.int32)
    others = ((frame + shift) % FRAMES) ^ swap
    ranks = jnp.sum(jnp.where(others[:, None] == ids[None, :], frame_order[None, :], 0), axis=1)
    chosen = [
        lax.dynamic_index_in_dim(mod_table, level + step, 0, keepdims=False)
        for step in range(STEPS)
    ]
    core = frame % 2
    blocks = gathered(tokens)
    source, blocks[4] = lax.optimization_barrier((jnp.transpose(qkv_weight, (1, 0, 2)), blocks[4]))
    weights = load(source, where)
    out_own, blocks[4] = lax.optimization_barrier((out_pieces(out_weight, core), blocks[4]))
    own_hidden = None
    out_weights = None
    attended = None
    for step_index in range(STEPS):
        mod_rows = chosen[step_index]
        if step_index == 0:
            q, kv, own_hidden = project_rows(blocks, where, mod_rows, weights)
        else:
            q, kv = project_columns(blocks, where, mod_rows, weights)
        queries = [
            q,
            over_frame(q, lambda f: f + 4),
            over_frame(q, lambda f: f - 4),
            over_frame(q, lambda f: f + 8),
        ]
        beside, queries[1], queries[2] = lax.optimization_barrier(
            (over_frame(kv, lambda f: f ^ 2), queries[1], queries[2])
        )
        kvs = [
            kv,
            beside,
            over_frame(kv, lambda f: f ^ 1),
            over_frame(beside, lambda f: f ^ 1),
        ]
        if step_index == 0:
            out_own, queries, kvs = lax.optimization_barrier((out_own, queries, kvs))
            out_mine = lax.all_to_all(out_own, "dp", 0, 0, tiled=True)
        own, own_sum, low, high, far = attend(queries, kvs, ranks)
        got = [
            over_frame(low, lambda f: f - 4),
            over_frame(high, lambda f: f + 4),
            over_frame(far, lambda f: f + 8),
        ]
        if step_index == 0:
            out_mine, got = lax.optimization_barrier((out_mine, got))
            out_weights = out_columns(out_mine, core)
        attended = finish(own, own_sum, got, where)
        own_hidden = add_branch(gathered(attended), out_weights, own_hidden, mod_rows, where)
        if step_index < STEPS - 1:
            blocks = gathered(own_hidden)
    pieces = own_hidden.reshape(GROUP, own_rows, width // GROUP)
    pieces = lax.all_to_all(pieces, "dp", 0, 0, tiled=True)
    hidden = jnp.transpose(pieces, (1, 0, 2)).reshape(own_rows, width)
    return (hidden, attended)


def solution(mesh):
    return jax.shard_map(
        per_device,
        mesh=mesh,
        in_specs=(P(("frame", "dp"), None), P(None, None, "dp"), P("dp", None), P(), P(), P()),
        out_specs=(P(("frame", "dp"), None), P("frame", "dp")),
        check_vma=False,
    )
```

```python
import functools
import math

import jax
import jax.numpy as jnp
import numpy as np
from jax import lax
from jax.experimental import pallas as pl
from jax.experimental.pallas import tpu as pltpu
from jax.sharding import PartitionSpec as P

HEAD = 128
STEPS = 2
EPSILON = 1e-06
ROWS = 16
BAND = 96
GROUP = 8
FRAMES = 16


def over_dp(value, to):
    return lax.ppermute(value, "dp", [(d, to(d) % GROUP) for d in range(GROUP)])


def over_frame(value, to):
    return lax.ppermute(value, "frame", [(f, to(f) % FRAMES) for f in range(FRAMES)])


def gathered(block):
    beside = over_dp(block, lambda d: d ^ 1)
    below = over_dp(block, lambda d: d + 2)
    above = over_dp(block, lambda d: d - 2)
    across = over_dp(block, lambda d: d + 4)
    beside_below = over_dp(beside, lambda d: d + 2)
    beside_above = over_dp(beside, lambda d: d - 2)
    beside_across = over_dp(across, lambda d: d ^ 1)
    return [block, beside, below, above, across, beside_below, beside_above, beside_across]


def origins(d):
    swap = np.array([0, 1, 0, 0, 0, 1, 1, 1], np.int32)
    shift = np.array([0, 0, 6, 2, 4, 6, 2, 4], np.int32)
    return ((d ^ swap) + shift) % GROUP


CHUNKS = 4


def local_call(kernel, name, info, operands, outs, scratch=(), limit=16, flops=0, moved=0):
    placed = [pltpu.with_memory_space_constraint(value, pltpu.VMEM) for value in operands]
    in_vmem = pl.BlockSpec(memory_space=pltpu.VMEM)
    return pl.pallas_call(
        kernel,
        out_shape=[pltpu.VMEM(shape, kind) for shape, kind in outs],
        in_specs=[pl.BlockSpec(memory_space=pltpu.SMEM)] + [in_vmem] * len(operands),
        out_specs=[in_vmem] * len(outs),
        scratch_shapes=list(scratch),
        compiler_params=pltpu.CompilerParams(vmem_limit_bytes=limit * 1024 * 1024),
        cost_estimate=pl.CostEstimate(flops=flops, bytes_accessed=moved, transcendentals=0),
        name=name,
    )(info, *placed)


def load_kernel(info, source, target, sems):
    del info
    copies = []
    for part in range(GROUP):
        span = source.shape[1] // GROUP
        cut = pl.ds(part * span, span)
        copies.append(
            pltpu.make_async_copy(source.at[:, cut, :], target.at[:, cut, :], sems.at[part])
        )
        copies[-1].start()
    for copy in copies:
        copy.wait()


def load(weights, info):
    return pl.pallas_call(
        load_kernel,
        out_shape=pltpu.VMEM(weights.shape, weights.dtype),
        in_specs=[pl.BlockSpec(memory_space=pltpu.SMEM), pl.BlockSpec(memory_space=pl.ANY)],
        out_specs=pl.BlockSpec(memory_space=pltpu.VMEM),
        scratch_shapes=[pltpu.SemaphoreType.DMA((GROUP,))],
        compiler_params=pltpu.CompilerParams(vmem_limit_bytes=2 * 1024 * 1024),
        cost_estimate=pl.CostEstimate(flops=0, bytes_accessed=2 * weights.size, transcendentals=0),
        name="load",
    )(info, pltpu.with_memory_space_constraint(weights, pltpu.HBM))


EARLY = 5


def folded(values):
    return sum(values[:, low : low + HEAD] for low in range(0, values.shape[1], HEAD))


def moments(parts, pivot):
    shifted = [part - pivot for part in parts]
    return folded(sum(shifted)), folded(sum(part * part for part in shifted))


def keep_moments(mean_ref, factor_ref, band, pivot, first, second, full):
    first = jnp.sum(first, axis=-1, keepdims=True) / full
    second = jnp.sum(second, axis=-1, keepdims=True) / full
    variance = second - first * first
    shape = (variance.shape[0], HEAD)
    mean_ref[band, :] = jnp.broadcast_to(pivot + first, shape)
    factor_ref[band, :] = jnp.broadcast_to(lax.rsqrt(variance + EPSILON), shape)


def normed(values, mean, factor, mod_ref, place):
    centered = values.astype(jnp.float32) - mean
    return (centered * factor * (1.0 + mod_ref[1:2, place]) + mod_ref[0:1, place]).astype(
        jnp.bfloat16
    )


def products(norm, chunks, weight):
    norm(0)
    totals = [None] * 3
    for chunk in range(CHUNKS):
        if chunk + 1 < CHUNKS:
            norm(chunk + 1)
        for which in range(3):
            term = jnp.dot(
                chunks[chunk][...], weight(which, chunk), preferred_element_type=jnp.float32
            )
            totals[which] = term if chunk == 0 else totals[which] + term
    return totals


def head_normed(values):
    blocks = []
    for low in range(0, values.shape[1], HEAD):
        block = values[:, low : low + HEAD]
        blocks.append(
            block * lax.rsqrt(jnp.mean(block * block, axis=-1, keepdims=True) + EPSILON)
        )
    return jnp.concatenate(blocks, axis=1).astype(jnp.bfloat16)


def rows_projected(blocks, mod_ref, w_ref, mean_ref, factor_ref, chunks):
    own_rows, full = blocks[0].shape
    width = full // GROUP
    span = full // CHUNKS
    for index, block in enumerate(blocks):
        rows = block[...].astype(jnp.float32)
        parts = [rows[:, chunk * width : (chunk + 1) * width] for chunk in range(GROUP)]
        pivot = jnp.mean(parts[0], axis=-1, keepdims=True)
        keep_moments(
            mean_ref,
            factor_ref,
            slice(index * own_rows, (index + 1) * own_rows),
            pivot,
            *moments(parts, pivot),
            full,
        )

    def norm(chunk):
        cut = slice(chunk * span, (chunk + 1) * span)
        for index, block in enumerate(blocks):
            band = slice(index * own_rows, (index + 1) * own_rows)
            chunks[chunk][band, :] = normed(
                block[:, cut], mean_ref[band, :1], factor_ref[band, :1], mod_ref, cut
            )

    totals = products(
        norm, chunks, lambda which, chunk: w_ref[which, chunk * span : (chunk + 1) * span, :]
    )
    return head_normed(totals[0]), head_normed(totals[1]), totals[2].astype(jnp.bfloat16)


def rows_early_kernel(info, *refs):
    del info
    blocks, (mod_ref, w_ref, out_ref, mean_ref, factor_ref) = refs[:EARLY], refs[EARLY:-CHUNKS]
    found = rows_projected(blocks, mod_ref, w_ref, mean_ref, factor_ref, refs[-CHUNKS:])
    for which in range(3):
        out_ref[which] = found[which]


def rows_late_kernel(info, *refs):
    blocks, rest = refs[:GROUP], refs[GROUP:-CHUNKS]
    mod_ref, w_ref, early_ref, q_ref, kv_ref, own_ref, mean_ref, factor_ref = rest
    found = rows_projected(blocks[EARLY:], mod_ref, w_ref, mean_ref, factor_ref, refs[-CHUNKS:])
    own_rows = blocks[0].shape[0]
    width = own_ref.shape[1]
    columns = pl.ds(pl.multiple_of(info[0] * width, HEAD), width)
    for index, block in enumerate(blocks):
        place = pl.ds(pl.multiple_of(info[index] * own_rows, ROWS), own_rows)
        own_ref[place, :] = block[:, columns]
        if index < EARLY:
            band = slice(index * own_rows, (index + 1) * own_rows)
            q_ref[place, :] = early_ref[0, band, :]
            kv_ref[0, place, :] = early_ref[1, band, :]
            kv_ref[1, place, :] = early_ref[2, band, :]
        else:
            band = slice((index - EARLY) * own_rows, (index - EARLY + 1) * own_rows)
            q_ref[place, :] = found[0][band]
            kv_ref[0, place, :] = found[1][band]
            kv_ref[1, place, :] = found[2][band]


def project_rows(blocks, info, mod_rows, weights):
    full, inner = weights.shape[1:]
    own_rows = blocks[0].shape[0]
    rows = own_rows * GROUP
    scratch = lambda count: (
        [pltpu.VMEM((count * own_rows, HEAD), jnp.float32)] * 2
        + [pltpu.VMEM((count * own_rows, full // CHUNKS), jnp.bfloat16)] * CHUNKS
    )
    early = local_call(
        rows_early_kernel,
        "rows_early",
        info,
        [*blocks[:EARLY], mod_rows, weights],
        [((3, EARLY * own_rows, inner), jnp.bfloat16)],
        scratch(EARLY),
        flops=6 * EARLY * own_rows * full * inner,
        moved=6 * full * inner,
    )[0]
    return local_call(
        rows_late_kernel,
        "rows_late",
        info,
        [*blocks, mod_rows, weights, early],
        [
            ((rows, inner), jnp.bfloat16),
            ((2, rows, inner), jnp.bfloat16),
            ((rows, full // GROUP), jnp.bfloat16),
        ],
        scratch(GROUP - EARLY),
        flops=6 * (GROUP - EARLY) * own_rows * full * inner,
        moved=6 * full * inner,
    )


def moments_kernel(info, *refs):
    del info
    blocks, out_ref = refs[:EARLY], refs[EARLY]
    rows = blocks[0].shape[0]

    for low in range(0, rows, BAND):
        band = slice(low, low + BAND)
        parts = [block[band, :].astype(jnp.float32) for block in blocks]
        pivot = jnp.mean(parts[0], axis=-1, keepdims=True)
        out_ref[0, band, :] = jnp.broadcast_to(pivot, (BAND, HEAD))
        out_ref[1, band, :], out_ref[2, band, :] = moments(parts, pivot)


def columns_kernel(info, *refs):
    blocks, rest, chunks = refs[:GROUP], refs[GROUP:-CHUNKS], refs[-CHUNKS:]
    mod_ref, w_ref, early_ref, q_ref, kv_ref, mean_ref, factor_ref = rest
    rows, width = blocks[0].shape
    full = width * GROUP
    each = GROUP // CHUNKS

    for low in range(0, rows, BAND):
        band = slice(low, low + BAND)
        pivot = early_ref[0, band, :1]
        first, second = moments(
            [block[band, :].astype(jnp.float32) for block in blocks[EARLY:]], pivot
        )
        keep_moments(
            mean_ref,
            factor_ref,
            band,
            pivot,
            first + early_ref[1, band, :],
            second + early_ref[2, band, :],
            full,
        )

    place = lambda index: pl.ds(pl.multiple_of(info[index] * width, HEAD), width)

    def norm(chunk):
        for part in range(each):
            index = chunk * each + part
            chunks[chunk][:, part * width : (part + 1) * width] = normed(
                blocks[index][...], mean_ref[:, :1], factor_ref[:, :1], mod_ref, place(index)
            )

    def weight(which, chunk):
        return jnp.concatenate(
            [w_ref[which, place(chunk * each + part), :] for part in range(each)], axis=0
        )

    totals = products(norm, chunks, weight)
    q_ref[...] = head_normed(totals[0])
    kv_ref[0] = head_normed(totals[1])
    kv_ref[1] = totals[2].astype(jnp.bfloat16)


def project_columns(blocks, info, mod_rows, weights):
    full, inner = weights.shape[1:]
    rows = blocks[0].shape[0]
    early = local_call(
        moments_kernel,
        "moments",
        info,
        blocks[:EARLY],
        [((3, rows, HEAD), jnp.float32)],
        flops=rows * full,
        moved=2 * EARLY * blocks[0].size,
    )[0]
    return local_call(
        columns_kernel,
        "columns",
        info,
        [*blocks, mod_rows, weights, early],
        [((rows, inner), jnp.bfloat16), ((2, rows, inner), jnp.bfloat16)],
        [pltpu.VMEM((rows, HEAD), jnp.float32)] * 2
        + [pltpu.VMEM((rows, full // CHUNKS), jnp.bfloat16)] * CHUNKS,
        flops=6 * rows * full * inner,
        moved=6 * full * inner,
    )


def add_pair(query, kv, total_ref):
    factor = math.log2(math.e) / math.sqrt(HEAD)
    heads = [slice(low, low + HEAD) for low in range(0, query.shape[1], HEAD)]
    weights = []
    for cut in heads:
        scores = lax.dot_general(
            query[:, cut],
            kv[0, :, cut],
            (((1,), (1,)), ((), ())),
            preferred_element_type=jnp.float32,
        )
        weights.append(jnp.exp2(scores * factor).astype(jnp.bfloat16))
    for head, cut in enumerate(heads):
        values = kv[1, :, cut]
        total_ref[head] += jnp.dot(
            weights[head],
            jnp.concatenate([values, jnp.ones_like(values)], axis=1),
            preferred_element_type=jnp.float32,
        )


def attend_kernel(frames, info, *refs):
    count = len(frames)
    queries, kvs, outs, total = refs[:count], refs[count : count + 4], refs[count + 4 : -1], refs[-1]
    rows, inner = queries[0].shape
    heads = inner // HEAD
    lanes = lax.broadcasted_iota(jnp.int32, (rows, HEAD), 1)
    for index, frame in enumerate(frames):
        total[...] = jnp.zeros_like(total)
        for which, kv in enumerate(kvs):

            @pl.when(info[4 + which] <= info[frame])
            def _(index=index, kv=kv):
                add_pair(queries[index], kv, total)

        sums = jnp.zeros((rows, HEAD), jnp.float32)
        for head in range(heads):
            cut = slice(head * HEAD, (head + 1) * HEAD)
            numerator, row_total = total[head, :, :HEAD], total[head, :, HEAD:]
            if frame == 0:
                outs[0][:, cut] = numerator
                sums = jnp.where(lanes == head, row_total, sums)
            else:
                outs[index][:rows, cut] = numerator.astype(jnp.bfloat16)
                coarse = row_total.astype(jnp.bfloat16).astype(jnp.float32)
                sums = jnp.where(lanes == head, coarse, sums)
                sums = jnp.where(lanes == heads + head, row_total - coarse, sums)
        if frame == 0:
            outs[1][...] = sums
        else:
            outs[index][rows:, :] = sums.T[:ROWS].astype(jnp.bfloat16)


def attend(frames, queries, kvs, info):
    rows, inner = queries[0].shape
    outs = (
        [((rows, inner), jnp.float32), ((rows, HEAD), jnp.float32)]
        if frames[0] == 0
        else [((rows + ROWS, inner), jnp.bfloat16)] * len(frames)
    )
    return local_call(
        functools.partial(attend_kernel, frames),
        "attend",
        info,
        [*(queries[frame] for frame in frames), *kvs],
        outs,
        [pltpu.VMEM((inner // HEAD, rows, 2 * HEAD), jnp.float32)],
        limit=8,
        flops=16 * len(frames) * rows * rows * inner,
        moved=32 * rows * inner,
    )


def finish_kernel(info, own_ref, own_sum_ref, *refs):
    del info
    got, out_ref = refs[:3], refs[3]
    rows, inner = own_ref.shape
    heads = inner // HEAD
    pairs = sum(ref[rows:, :].astype(jnp.float32) for ref in got)
    pairs = jnp.concatenate([pairs, jnp.zeros((HEAD - ROWS, inner), jnp.float32)], axis=0).T
    for head in range(heads):
        cut = slice(head * HEAD, (head + 1) * HEAD)
        row_total = (
            own_sum_ref[:, head : head + 1]
            + pairs[:, head : head + 1]
            + pairs[:, heads + head : heads + head + 1]
        )
        numerator = own_ref[:, cut] + sum(ref[:rows, cut].astype(jnp.float32) for ref in got)
        out_ref[:, cut] = (numerator / row_total).astype(jnp.bfloat16)


def finish(own, own_sum, got, info):
    return local_call(
        finish_kernel,
        "finish",
        info,
        [own, own_sum, *got],
        [(own.shape, jnp.bfloat16)],
    )[0]


def early_kernel(info, *refs):
    parts, (w_ref, out_ref) = refs[:EARLY], refs[EARLY:]
    out_ref[...] = sum(
        jnp.dot(part[...], w_ref[info[index]], preferred_element_type=jnp.float32)
        for index, part in enumerate(parts)
    )


def late_kernel(info, *refs):
    count = GROUP - EARLY
    parts, (sum_ref, w_ref, hidden_ref, mod_ref, out_ref) = refs[:count], refs[count:]
    width = hidden_ref.shape[1]
    total = sum_ref[...] + sum(
        jnp.dot(part[...], w_ref[info[EARLY + index]], preferred_element_type=jnp.float32)
        for index, part in enumerate(parts)
    )
    columns = pl.ds(pl.multiple_of(info[0] * width, HEAD), width)
    out_ref[...] = (hidden_ref[...].astype(jnp.float32) + mod_ref[2:3, columns] * total).astype(
        jnp.bfloat16
    )


def add_branch(parts, weights, hidden, mod_rows, info):
    rows, inner = parts[0].shape
    each = 2 * rows * inner * hidden.shape[1]
    moved = 4 * hidden.size
    early = local_call(
        early_kernel,
        "early",
        info,
        [*parts[:EARLY], weights],
        [(hidden.shape, jnp.float32)],
        flops=EARLY * each,
        moved=moved,
    )[0]
    return local_call(
        late_kernel,
        "late",
        info,
        [*parts[EARLY:], early, weights, hidden, mod_rows],
        [(hidden.shape, jnp.bfloat16)],
        flops=(GROUP - EARLY) * each,
        moved=moved,
    )[0]


def out_pieces(out_weight, core):
    rows, width = out_weight.shape
    half = rows // 2
    own = lax.dynamic_slice(out_weight, (core * half, 0), (half, width))
    return jnp.transpose(own.reshape(half, GROUP, width // GROUP), (1, 0, 2))


def out_columns(mine, core):
    theirs = over_frame(mine, lambda f: f ^ 1)
    first = core == 0
    return jnp.concatenate(
        [jnp.where(first, mine, theirs), jnp.where(first, theirs, mine)], axis=1
    )


def per_device(tokens, qkv_weight, out_weight, mod_table, levels, frame_order):
    own_rows, width = tokens.shape
    frame = lax.axis_index("frame")
    ids = jnp.arange(FRAMES, dtype=jnp.int32)
    level = jnp.sum(jnp.where(ids == frame, levels, 0))
    where = origins(lax.axis_index("dp")).astype(jnp.int32)
    shift = np.array([0, 12, 4, 8, 0, 0, 0, 0], np.int32)
    swap = np.array([0, 0, 0, 0, 0, 1, 2, 3], np.int32)
    others = ((frame + shift) % FRAMES) ^ swap
    ranks = jnp.sum(jnp.where(others[:, None] == ids[None, :], frame_order[None, :], 0), axis=1)
    chosen = [
        lax.dynamic_index_in_dim(mod_table, level + step, 0, keepdims=False)
        for step in range(STEPS)
    ]
    core = frame % 2
    blocks = gathered(tokens)
    source, blocks[4] = lax.optimization_barrier((jnp.transpose(qkv_weight, (1, 0, 2)), blocks[4]))
    weights = load(source, where)
    out_own, blocks[4] = lax.optimization_barrier((out_pieces(out_weight, core), blocks[4]))
    own_hidden = None
    out_weights = None
    attended = None
    for step_index in range(STEPS):
        mod_rows = chosen[step_index]
        if step_index == 0:
            q, kv, own_hidden = project_rows(blocks, where, mod_rows, weights)
        else:
            q, kv = project_columns(blocks, where, mod_rows, weights)
        queries = [
            q,
            over_frame(q, lambda f: f + 4),
            over_frame(q, lambda f: f - 4),
            over_frame(q, lambda f: f + 8),
        ]
        beside = over_frame(kv, lambda f: f ^ 2)
        mate = over_frame(kv, lambda f: f ^ 1)
        beside, queries[1], queries[2], queries[3] = lax.optimization_barrier(
            (beside, queries[1], queries[2], queries[3])
        )
        beside_mate = over_frame(beside, lambda f: f ^ 1)
        kvs = [kv, mate, beside, beside_mate]
        (far,) = attend([3], queries, kvs, ranks)
        low, high = attend([1, 2], queries, kvs, ranks)
        own, own_sum = attend([0], queries, kvs, ranks)
        if step_index == 0:
            out_own, own_sum = lax.optimization_barrier((out_own, own_sum))
            out_mine = lax.all_to_all(out_own, "dp", 0, 0, tiled=True)
        got = [
            over_frame(far, lambda f: f + 8),
            over_frame(low, lambda f: f - 4),
            over_frame(high, lambda f: f + 4),
        ]
        if step_index == 0:
            out_mine, got = lax.optimization_barrier((out_mine, got))
            out_weights = out_columns(out_mine, core)
        attended = finish(own, own_sum, got, where)
        own_hidden = add_branch(gathered(attended), out_weights, own_hidden, mod_rows, where)
        if step_index < STEPS - 1:
            blocks = gathered(own_hidden)
    pieces = own_hidden.reshape(GROUP, own_rows, width // GROUP)
    pieces = lax.all_to_all(pieces, "dp", 0, 0, tiled=True)
    hidden = jnp.transpose(pieces, (1, 0, 2)).reshape(own_rows, width)
    return (hidden, attended)


def solution(mesh):
    return jax.shard_map(
        per_device,
        mesh=mesh,
        in_specs=(P(("frame", "dp"), None), P(None, None, "dp"), P("dp", None), P(), P(), P()),
        out_specs=(P(("frame", "dp"), None), P("frame", "dp")),
        check_vma=False,
    )
```

```python
import functools
import math

import jax
import jax.numpy as jnp
import numpy as np
from jax import lax
from jax.experimental import pallas as pl
from jax.experimental.pallas import tpu as pltpu
from jax.sharding import PartitionSpec as P

HEAD = 128
STEPS = 2
EPSILON = 1e-06
ROWS = 16
BAND = 96
GROUP = 8
FRAMES = 16


def over_dp(value, to):
    return lax.ppermute(value, "dp", [(d, to(d) % GROUP) for d in range(GROUP)])


def over_frame(value, to):
    return lax.ppermute(value, "frame", [(f, to(f) % FRAMES) for f in range(FRAMES)])


def gathered(block):
    beside = over_dp(block, lambda d: d ^ 1)
    below = over_dp(block, lambda d: d + 2)
    above = over_dp(block, lambda d: d - 2)
    across = over_dp(block, lambda d: d + 4)
    beside_below = over_dp(beside, lambda d: d + 2)
    beside_above = over_dp(beside, lambda d: d - 2)
    beside_across = over_dp(across, lambda d: d ^ 1)
    return [block, beside, below, above, across, beside_below, beside_above, beside_across]


def origins(d):
    swap = np.array([0, 1, 0, 0, 0, 1, 1, 1], np.int32)
    shift = np.array([0, 0, 6, 2, 4, 6, 2, 4], np.int32)
    return ((d ^ swap) + shift) % GROUP


CHUNKS = 4


def local_call(kernel, name, info, operands, outs, scratch=(), limit=16, flops=0, moved=0):
    placed = [pltpu.with_memory_space_constraint(value, pltpu.VMEM) for value in operands]
    in_vmem = pl.BlockSpec(memory_space=pltpu.VMEM)
    return pl.pallas_call(
        kernel,
        out_shape=[pltpu.VMEM(shape, kind) for shape, kind in outs],
        in_specs=[pl.BlockSpec(memory_space=pltpu.SMEM)] + [in_vmem] * len(operands),
        out_specs=[in_vmem] * len(outs),
        scratch_shapes=list(scratch),
        compiler_params=pltpu.CompilerParams(vmem_limit_bytes=limit * 1024 * 1024),
        cost_estimate=pl.CostEstimate(flops=flops, bytes_accessed=moved, transcendentals=0),
        name=name,
    )(info, *placed)


def load_kernel(info, source, target, sems):
    del info
    copies = []
    for part in range(GROUP):
        span = source.shape[1] // GROUP
        cut = pl.ds(part * span, span)
        copies.append(
            pltpu.make_async_copy(source.at[:, cut, :], target.at[:, cut, :], sems.at[part])
        )
        copies[-1].start()
    for copy in copies:
        copy.wait()


def load(weights, info):
    return pl.pallas_call(
        load_kernel,
        out_shape=pltpu.VMEM(weights.shape, weights.dtype),
        in_specs=[pl.BlockSpec(memory_space=pltpu.SMEM), pl.BlockSpec(memory_space=pl.ANY)],
        out_specs=pl.BlockSpec(memory_space=pltpu.VMEM),
        scratch_shapes=[pltpu.SemaphoreType.DMA((GROUP,))],
        compiler_params=pltpu.CompilerParams(vmem_limit_bytes=2 * 1024 * 1024),
        cost_estimate=pl.CostEstimate(flops=0, bytes_accessed=2 * weights.size, transcendentals=0),
        name="load",
    )(info, pltpu.with_memory_space_constraint(weights, pltpu.HBM))


EARLY = 5


def folded(values):
    return sum(values[:, low : low + HEAD] for low in range(0, values.shape[1], HEAD))


def moments(parts, pivot):
    shifted = [part - pivot for part in parts]
    return folded(sum(shifted)), folded(sum(part * part for part in shifted))


def keep_moments(mean_ref, factor_ref, band, pivot, first, second, full):
    first = jnp.sum(first, axis=-1, keepdims=True) / full
    second = jnp.sum(second, axis=-1, keepdims=True) / full
    variance = second - first * first
    shape = (variance.shape[0], HEAD)
    mean_ref[band, :] = jnp.broadcast_to(pivot + first, shape)
    factor_ref[band, :] = jnp.broadcast_to(lax.rsqrt(variance + EPSILON), shape)


def normed(values, mean, factor, mod_ref, place):
    centered = values.astype(jnp.float32) - mean
    return (centered * factor * (1.0 + mod_ref[1:2, place]) + mod_ref[0:1, place]).astype(
        jnp.bfloat16
    )


def products(norm, chunks, weight):
    norm(0)
    totals = [None] * 3
    for chunk in range(CHUNKS):
        if chunk + 1 < CHUNKS:
            norm(chunk + 1)
        for which in range(3):
            term = jnp.dot(
                chunks[chunk][...], weight(which, chunk), preferred_element_type=jnp.float32
            )
            totals[which] = term if chunk == 0 else totals[which] + term
    return totals


def head_normed(values):
    blocks = []
    for low in range(0, values.shape[1], HEAD):
        block = values[:, low : low + HEAD]
        blocks.append(
            block * lax.rsqrt(jnp.mean(block * block, axis=-1, keepdims=True) + EPSILON)
        )
    return jnp.concatenate(blocks, axis=1).astype(jnp.bfloat16)


def rows_projected(blocks, mod_ref, w_ref, mean_ref, factor_ref, chunks):
    own_rows, full = blocks[0].shape
    width = full // GROUP
    span = full // CHUNKS
    for index, block in enumerate(blocks):
        rows = block[...].astype(jnp.float32)
        parts = [rows[:, chunk * width : (chunk + 1) * width] for chunk in range(GROUP)]
        pivot = jnp.mean(parts[0], axis=-1, keepdims=True)
        keep_moments(
            mean_ref,
            factor_ref,
            slice(index * own_rows, (index + 1) * own_rows),
            pivot,
            *moments(parts, pivot),
            full,
        )

    def norm(chunk):
        cut = slice(chunk * span, (chunk + 1) * span)
        for index, block in enumerate(blocks):
            band = slice(index * own_rows, (index + 1) * own_rows)
            chunks[chunk][band, :] = normed(
                block[:, cut], mean_ref[band, :1], factor_ref[band, :1], mod_ref, cut
            )

    totals = products(
        norm, chunks, lambda which, chunk: w_ref[which, chunk * span : (chunk + 1) * span, :]
    )
    return head_normed(totals[0]), head_normed(totals[1]), totals[2].astype(jnp.bfloat16)


def rows_early_kernel(info, *refs):
    del info
    blocks, (mod_ref, w_ref, out_ref, mean_ref, factor_ref) = refs[:EARLY], refs[EARLY:-CHUNKS]
    found = rows_projected(blocks, mod_ref, w_ref, mean_ref, factor_ref, refs[-CHUNKS:])
    for which in range(3):
        out_ref[which] = found[which]


def rows_late_kernel(info, *refs):
    blocks, rest = refs[:GROUP], refs[GROUP:-CHUNKS]
    mod_ref, w_ref, early_ref, q_ref, kv_ref, own_ref, mean_ref, factor_ref = rest
    found = rows_projected(blocks[EARLY:], mod_ref, w_ref, mean_ref, factor_ref, refs[-CHUNKS:])
    own_rows = blocks[0].shape[0]
    width = own_ref.shape[1]
    columns = pl.ds(pl.multiple_of(info[0] * width, HEAD), width)
    for index, block in enumerate(blocks):
        place = pl.ds(pl.multiple_of(info[index] * own_rows, ROWS), own_rows)
        own_ref[place, :] = block[:, columns]
        if index < EARLY:
            band = slice(index * own_rows, (index + 1) * own_rows)
            q_ref[place, :] = early_ref[0, band, :]
            kv_ref[0, place, :] = early_ref[1, band, :]
            kv_ref[1, place, :] = early_ref[2, band, :]
        else:
            band = slice((index - EARLY) * own_rows, (index - EARLY + 1) * own_rows)
            q_ref[place, :] = found[0][band]
            kv_ref[0, place, :] = found[1][band]
            kv_ref[1, place, :] = found[2][band]


def project_rows(blocks, info, mod_rows, weights):
    full, inner = weights.shape[1:]
    own_rows = blocks[0].shape[0]
    rows = own_rows * GROUP
    scratch = lambda count: (
        [pltpu.VMEM((count * own_rows, HEAD), jnp.float32)] * 2
        + [pltpu.VMEM((count * own_rows, full // CHUNKS), jnp.bfloat16)] * CHUNKS
    )
    early = local_call(
        rows_early_kernel,
        "rows_early",
        info,
        [*blocks[:EARLY], mod_rows, weights],
        [((3, EARLY * own_rows, inner), jnp.bfloat16)],
        scratch(EARLY),
        flops=6 * EARLY * own_rows * full * inner,
        moved=6 * full * inner,
    )[0]
    return local_call(
        rows_late_kernel,
        "rows_late",
        info,
        [*blocks, mod_rows, weights, early],
        [
            ((rows, inner), jnp.bfloat16),
            ((2, rows, inner), jnp.bfloat16),
            ((rows, full // GROUP), jnp.bfloat16),
        ],
        scratch(GROUP - EARLY),
        flops=6 * (GROUP - EARLY) * own_rows * full * inner,
        moved=6 * full * inner,
    )


def moments_kernel(info, *refs):
    del info
    blocks, out_ref = refs[:EARLY], refs[EARLY]
    rows = blocks[0].shape[0]

    for low in range(0, rows, BAND):
        band = slice(low, low + BAND)
        parts = [block[band, :].astype(jnp.float32) for block in blocks]
        pivot = jnp.mean(parts[0], axis=-1, keepdims=True)
        out_ref[0, band, :] = jnp.broadcast_to(pivot, (BAND, HEAD))
        out_ref[1, band, :], out_ref[2, band, :] = moments(parts, pivot)


def columns_kernel(info, *refs):
    blocks, rest, chunks = refs[:GROUP], refs[GROUP:-CHUNKS], refs[-CHUNKS:]
    mod_ref, w_ref, early_ref, q_ref, kv_ref, mean_ref, factor_ref = rest
    rows, width = blocks[0].shape
    full = width * GROUP
    each = GROUP // CHUNKS

    for low in range(0, rows, BAND):
        band = slice(low, low + BAND)
        pivot = early_ref[0, band, :1]
        first, second = moments(
            [block[band, :].astype(jnp.float32) for block in blocks[EARLY:]], pivot
        )
        keep_moments(
            mean_ref,
            factor_ref,
            band,
            pivot,
            first + early_ref[1, band, :],
            second + early_ref[2, band, :],
            full,
        )

    place = lambda index: pl.ds(pl.multiple_of(info[index] * width, HEAD), width)

    def norm(chunk):
        for part in range(each):
            index = chunk * each + part
            chunks[chunk][:, part * width : (part + 1) * width] = normed(
                blocks[index][...], mean_ref[:, :1], factor_ref[:, :1], mod_ref, place(index)
            )

    def weight(which, chunk):
        return jnp.concatenate(
            [w_ref[which, place(chunk * each + part), :] for part in range(each)], axis=0
        )

    totals = products(norm, chunks, weight)
    q_ref[...] = head_normed(totals[0])
    kv_ref[0] = head_normed(totals[1])
    kv_ref[1] = totals[2].astype(jnp.bfloat16)


def project_columns(blocks, info, mod_rows, weights):
    full, inner = weights.shape[1:]
    rows = blocks[0].shape[0]
    early = local_call(
        moments_kernel,
        "moments",
        info,
        blocks[:EARLY],
        [((3, rows, HEAD), jnp.float32)],
        flops=rows * full,
        moved=2 * EARLY * blocks[0].size,
    )[0]
    return local_call(
        columns_kernel,
        "columns",
        info,
        [*blocks, mod_rows, weights, early],
        [((rows, inner), jnp.bfloat16), ((2, rows, inner), jnp.bfloat16)],
        [pltpu.VMEM((rows, HEAD), jnp.float32)] * 2
        + [pltpu.VMEM((rows, full // CHUNKS), jnp.bfloat16)] * CHUNKS,
        flops=6 * rows * full * inner,
        moved=6 * full * inner,
    )


def add_pair(query, kv, total_ref):
    factor = math.log2(math.e) / math.sqrt(HEAD)
    heads = [slice(low, low + HEAD) for low in range(0, query.shape[1], HEAD)]
    weights = []
    for cut in heads:
        scores = lax.dot_general(
            query[:, cut],
            kv[0, :, cut],
            (((1,), (1,)), ((), ())),
            preferred_element_type=jnp.float32,
        )
        weights.append(jnp.exp2(scores * factor).astype(jnp.bfloat16))
    for head, cut in enumerate(heads):
        values = kv[1, :, cut]
        total_ref[head] += jnp.dot(
            weights[head],
            jnp.concatenate([values, jnp.ones_like(values)], axis=1),
            preferred_element_type=jnp.float32,
        )


def attend_kernel(frames, info, *refs):
    count = len(frames)
    queries, kvs, rest = refs[:count], refs[count : count + 4], refs[count + 4 :]
    outs = rest[-4:-2] if frames[0] == 0 else rest[-2 - count : -2]
    mark_ref, total = rest[-2:]
    mark_ref[...] = jnp.zeros_like(mark_ref)
    rows, inner = queries[0].shape
    heads = inner // HEAD
    lanes = lax.broadcasted_iota(jnp.int32, (rows, HEAD), 1)
    for index, frame in enumerate(frames):
        total[...] = jnp.zeros_like(total)
        for which, kv in enumerate(kvs):

            @pl.when(info[4 + which] <= info[frame])
            def _(index=index, kv=kv):
                add_pair(queries[index], kv, total)

        sums = jnp.zeros((rows, HEAD), jnp.float32)
        for head in range(heads):
            cut = slice(head * HEAD, (head + 1) * HEAD)
            numerator, row_total = total[head, :, :HEAD], total[head, :, HEAD:]
            if frame == 0:
                outs[0][:, cut] = numerator
                sums = jnp.where(lanes == head, row_total, sums)
            else:
                outs[index][:rows, cut] = numerator.astype(jnp.bfloat16)
                coarse = row_total.astype(jnp.bfloat16).astype(jnp.float32)
                sums = jnp.where(lanes == head, coarse, sums)
                sums = jnp.where(lanes == heads + head, row_total - coarse, sums)
        if frame == 0:
            outs[1][...] = sums
        else:
            outs[index][rows:, :] = sums.T[:ROWS].astype(jnp.bfloat16)


def attend(frames, queries, kvs, info, after=()):
    rows, inner = queries[0].shape
    outs = (
        [((rows, inner), jnp.float32), ((rows, HEAD), jnp.float32)]
        if frames[0] == 0
        else [((rows + ROWS, inner), jnp.bfloat16)] * len(frames)
    )
    return local_call(
        functools.partial(attend_kernel, frames),
        "attend",
        info,
        [*(queries[frame] for frame in frames), *kvs, *after],
        outs + [((8, HEAD), jnp.float32)],
        [pltpu.VMEM((inner // HEAD, rows, 2 * HEAD), jnp.float32)],
        limit=8,
        flops=16 * len(frames) * rows * rows * inner,
        moved=32 * rows * inner,
    )


def finish_kernel(info, own_ref, own_sum_ref, *refs):
    del info
    got, out_ref = refs[:3], refs[3]
    rows, inner = own_ref.shape
    heads = inner // HEAD
    pairs = sum(ref[rows:, :].astype(jnp.float32) for ref in got)
    pairs = jnp.concatenate([pairs, jnp.zeros((HEAD - ROWS, inner), jnp.float32)], axis=0).T
    for head in range(heads):
        cut = slice(head * HEAD, (head + 1) * HEAD)
        row_total = (
            own_sum_ref[:, head : head + 1]
            + pairs[:, head : head + 1]
            + pairs[:, heads + head : heads + head + 1]
        )
        numerator = own_ref[:, cut] + sum(ref[:rows, cut].astype(jnp.float32) for ref in got)
        out_ref[:, cut] = (numerator / row_total).astype(jnp.bfloat16)


def finish(own, own_sum, got, info):
    return local_call(
        finish_kernel,
        "finish",
        info,
        [own, own_sum, *got],
        [(own.shape, jnp.bfloat16)],
    )[0]


def early_kernel(info, *refs):
    parts, (w_ref, out_ref) = refs[:EARLY], refs[EARLY:]
    out_ref[...] = sum(
        jnp.dot(part[...], w_ref[info[index]], preferred_element_type=jnp.float32)
        for index, part in enumerate(parts)
    )


def late_kernel(info, *refs):
    count = GROUP - EARLY
    parts, (sum_ref, w_ref, hidden_ref, mod_ref, out_ref) = refs[:count], refs[count:]
    width = hidden_ref.shape[1]
    total = sum_ref[...] + sum(
        jnp.dot(part[...], w_ref[info[EARLY + index]], preferred_element_type=jnp.float32)
        for index, part in enumerate(parts)
    )
    columns = pl.ds(pl.multiple_of(info[0] * width, HEAD), width)
    out_ref[...] = (hidden_ref[...].astype(jnp.float32) + mod_ref[2:3, columns] * total).astype(
        jnp.bfloat16
    )


def add_branch(parts, weights, hidden, mod_rows, info):
    rows, inner = parts[0].shape
    each = 2 * rows * inner * hidden.shape[1]
    moved = 4 * hidden.size
    early = local_call(
        early_kernel,
        "early",
        info,
        [*parts[:EARLY], weights],
        [(hidden.shape, jnp.float32)],
        flops=EARLY * each,
        moved=moved,
    )[0]
    return local_call(
        late_kernel,
        "late",
        info,
        [*parts[EARLY:], early, weights, hidden, mod_rows],
        [(hidden.shape, jnp.bfloat16)],
        flops=(GROUP - EARLY) * each,
        moved=moved,
    )[0]


def out_pieces(out_weight, core):
    rows, width = out_weight.shape
    half = rows // 2
    own = lax.dynamic_slice(out_weight, (core * half, 0), (half, width))
    return jnp.transpose(own.reshape(half, GROUP, width // GROUP), (1, 0, 2))


def out_columns(mine, core):
    theirs = over_frame(mine, lambda f: f ^ 1)
    first = core == 0
    return jnp.concatenate(
        [jnp.where(first, mine, theirs), jnp.where(first, theirs, mine)], axis=1
    )


def per_device(tokens, qkv_weight, out_weight, mod_table, levels, frame_order):
    own_rows, width = tokens.shape
    frame = lax.axis_index("frame")
    ids = jnp.arange(FRAMES, dtype=jnp.int32)
    level = jnp.sum(jnp.where(ids == frame, levels, 0))
    where = origins(lax.axis_index("dp")).astype(jnp.int32)
    shift = np.array([0, 12, 4, 8, 0, 0, 0, 0], np.int32)
    swap = np.array([0, 0, 0, 0, 0, 1, 2, 3], np.int32)
    others = ((frame + shift) % FRAMES) ^ swap
    ranks = jnp.sum(jnp.where(others[:, None] == ids[None, :], frame_order[None, :], 0), axis=1)
    chosen = [
        lax.dynamic_index_in_dim(mod_table, level + step, 0, keepdims=False)
        for step in range(STEPS)
    ]
    core = frame % 2
    blocks = gathered(tokens)
    source, blocks[4] = lax.optimization_barrier((jnp.transpose(qkv_weight, (1, 0, 2)), blocks[4]))
    weights = load(source, where)
    out_own, blocks[4] = lax.optimization_barrier((out_pieces(out_weight, core), blocks[4]))
    own_hidden = None
    out_weights = None
    attended = None
    for step_index in range(STEPS):
        mod_rows = chosen[step_index]
        if step_index == 0:
            q, kv, own_hidden = project_rows(blocks, where, mod_rows, weights)
        else:
            q, kv = project_columns(blocks, where, mod_rows, weights)
        queries = [
            q,
            over_frame(q, lambda f: f + 4),
            over_frame(q, lambda f: f - 4),
            over_frame(q, lambda f: f + 8),
        ]
        beside = over_frame(kv, lambda f: f ^ 2)
        mate = over_frame(kv, lambda f: f ^ 1)
        beside, queries[1], queries[2], queries[3], out_own = lax.optimization_barrier(
            (beside, queries[1], queries[2], queries[3], out_own)
        )
        if step_index == 0:
            out_mine = lax.all_to_all(out_own, "dp", 0, 0, tiled=True)
            out_own = level
        beside_mate = over_frame(beside, lambda f: f ^ 1)
        kvs = [kv, mate, beside, beside_mate]
        far, mark = attend([3], queries, kvs, ranks)
        own, own_sum, mark = attend([0], queries, kvs, ranks, [mark])
        low, high, _ = attend([1, 2], queries, kvs, ranks, [mark])
        got = [
            over_frame(far, lambda f: f + 8),
            over_frame(low, lambda f: f - 4),
            over_frame(high, lambda f: f + 4),
        ]
        if step_index == 0:
            out_mine, got = lax.optimization_barrier((out_mine, got))
            out_weights = out_columns(out_mine, core)
        attended = finish(own, own_sum, got, where)
        own_hidden = add_branch(gathered(attended), out_weights, own_hidden, mod_rows, where)
        if step_index < STEPS - 1:
            blocks = gathered(own_hidden)
    pieces = own_hidden.reshape(GROUP, own_rows, width // GROUP)
    pieces = lax.all_to_all(pieces, "dp", 0, 0, tiled=True)
    hidden = jnp.transpose(pieces, (1, 0, 2)).reshape(own_rows, width)
    return (hidden, attended)


def solution(mesh):
    return jax.shard_map(
        per_device,
        mesh=mesh,
        in_specs=(P(("frame", "dp"), None), P(None, None, "dp"), P("dp", None), P(), P(), P()),
        out_specs=(P(("frame", "dp"), None), P("frame", "dp")),
        check_vma=False,
    )
```

```python
import functools
import math

import jax
import jax.numpy as jnp
import numpy as np
from jax import lax
from jax.experimental import pallas as pl
from jax.experimental.pallas import tpu as pltpu
from jax.sharding import PartitionSpec as P

HEAD = 128
STEPS = 2
EPSILON = 1e-06
ROWS = 16
BAND = 96
GROUP = 8
FRAMES = 16


def over_dp(value, to):
    return lax.ppermute(value, "dp", [(d, to(d) % GROUP) for d in range(GROUP)])


def over_frame(value, to):
    return lax.ppermute(value, "frame", [(f, to(f) % FRAMES) for f in range(FRAMES)])


def gathered(block):
    beside = over_dp(block, lambda d: d ^ 1)
    below = over_dp(block, lambda d: d + 2)
    above = over_dp(block, lambda d: d - 2)
    across = over_dp(block, lambda d: d + 4)
    beside_below = over_dp(beside, lambda d: d + 2)
    beside_above = over_dp(beside, lambda d: d - 2)
    beside_across = over_dp(across, lambda d: d ^ 1)
    return [block, beside, below, above, across, beside_below, beside_above, beside_across]


def origins(d):
    swap = np.array([0, 1, 0, 0, 0, 1, 1, 1], np.int32)
    shift = np.array([0, 0, 6, 2, 4, 6, 2, 4], np.int32)
    return ((d ^ swap) + shift) % GROUP


CHUNKS = 4


def local_call(kernel, name, info, operands, outs, scratch=(), limit=16, flops=0, moved=0):
    placed = [pltpu.with_memory_space_constraint(value, pltpu.VMEM) for value in operands]
    in_vmem = pl.BlockSpec(memory_space=pltpu.VMEM)
    return pl.pallas_call(
        kernel,
        out_shape=[pltpu.VMEM(shape, kind) for shape, kind in outs],
        in_specs=[pl.BlockSpec(memory_space=pltpu.SMEM)] + [in_vmem] * len(operands),
        out_specs=[in_vmem] * len(outs),
        scratch_shapes=list(scratch),
        compiler_params=pltpu.CompilerParams(vmem_limit_bytes=limit * 1024 * 1024),
        cost_estimate=pl.CostEstimate(flops=flops, bytes_accessed=moved, transcendentals=0),
        name=name,
    )(info, *placed)


def load_kernel(info, source, target, sems):
    del info
    copies = []
    for part in range(GROUP):
        span = source.shape[1] // GROUP
        cut = pl.ds(part * span, span)
        copies.append(
            pltpu.make_async_copy(source.at[:, cut, :], target.at[:, cut, :], sems.at[part])
        )
        copies[-1].start()
    for copy in copies:
        copy.wait()


def load(weights, info):
    return pl.pallas_call(
        load_kernel,
        out_shape=pltpu.VMEM(weights.shape, weights.dtype),
        in_specs=[pl.BlockSpec(memory_space=pltpu.SMEM), pl.BlockSpec(memory_space=pl.ANY)],
        out_specs=pl.BlockSpec(memory_space=pltpu.VMEM),
        scratch_shapes=[pltpu.SemaphoreType.DMA((GROUP,))],
        compiler_params=pltpu.CompilerParams(vmem_limit_bytes=2 * 1024 * 1024),
        cost_estimate=pl.CostEstimate(flops=0, bytes_accessed=2 * weights.size, transcendentals=0),
        name="load",
    )(info, pltpu.with_memory_space_constraint(weights, pltpu.HBM))


EARLY = 5


def folded(values):
    return sum(values[:, low : low + HEAD] for low in range(0, values.shape[1], HEAD))


def moments(parts, pivot):
    shifted = [part - pivot for part in parts]
    return folded(sum(shifted)), folded(sum(part * part for part in shifted))


def keep_moments(mean_ref, factor_ref, band, pivot, first, second, full):
    first = jnp.sum(first, axis=-1, keepdims=True) / full
    second = jnp.sum(second, axis=-1, keepdims=True) / full
    variance = second - first * first
    shape = (variance.shape[0], HEAD)
    mean_ref[band, :] = jnp.broadcast_to(pivot + first, shape)
    factor_ref[band, :] = jnp.broadcast_to(lax.rsqrt(variance + EPSILON), shape)


def normed(values, mean, factor, mod_ref, place):
    centered = values.astype(jnp.float32) - mean
    return (centered * factor * (1.0 + mod_ref[1:2, place]) + mod_ref[0:1, place]).astype(
        jnp.bfloat16
    )


def products(norm, chunks, weight, wanted=(0, 1, 2)):
    norm(0)
    totals = [None] * 3
    for chunk in range(CHUNKS):
        if chunk + 1 < CHUNKS:
            norm(chunk + 1)
        for which in wanted:
            term = jnp.dot(
                chunks[chunk][...], weight(which, chunk), preferred_element_type=jnp.float32
            )
            totals[which] = term if chunk == 0 else totals[which] + term
    return totals


def head_normed(values):
    blocks = []
    for low in range(0, values.shape[1], HEAD):
        block = values[:, low : low + HEAD]
        blocks.append(
            block * lax.rsqrt(jnp.mean(block * block, axis=-1, keepdims=True) + EPSILON)
        )
    return jnp.concatenate(blocks, axis=1).astype(jnp.bfloat16)


def rows_projected(blocks, mod_ref, w_ref, mean_ref, factor_ref, chunks):
    own_rows, full = blocks[0].shape
    width = full // GROUP
    span = full // CHUNKS
    for index, block in enumerate(blocks):
        rows = block[...].astype(jnp.float32)
        parts = [rows[:, chunk * width : (chunk + 1) * width] for chunk in range(GROUP)]
        pivot = jnp.mean(parts[0], axis=-1, keepdims=True)
        keep_moments(
            mean_ref,
            factor_ref,
            slice(index * own_rows, (index + 1) * own_rows),
            pivot,
            *moments(parts, pivot),
            full,
        )

    def norm(chunk):
        cut = slice(chunk * span, (chunk + 1) * span)
        for index, block in enumerate(blocks):
            band = slice(index * own_rows, (index + 1) * own_rows)
            chunks[chunk][band, :] = normed(
                block[:, cut], mean_ref[band, :1], factor_ref[band, :1], mod_ref, cut
            )

    totals = products(
        norm, chunks, lambda which, chunk: w_ref[which, chunk * span : (chunk + 1) * span, :]
    )
    return head_normed(totals[0]), head_normed(totals[1]), totals[2].astype(jnp.bfloat16)


def rows_early_kernel(info, *refs):
    del info
    blocks, (mod_ref, w_ref, out_ref, mean_ref, factor_ref) = refs[:EARLY], refs[EARLY:-CHUNKS]
    found = rows_projected(blocks, mod_ref, w_ref, mean_ref, factor_ref, refs[-CHUNKS:])
    for which in range(3):
        out_ref[which] = found[which]


def rows_late_kernel(info, *refs):
    blocks, rest = refs[:GROUP], refs[GROUP:-CHUNKS]
    mod_ref, w_ref, early_ref, q_ref, kv_ref, own_ref, mean_ref, factor_ref = rest
    found = rows_projected(blocks[EARLY:], mod_ref, w_ref, mean_ref, factor_ref, refs[-CHUNKS:])
    own_rows = blocks[0].shape[0]
    width = own_ref.shape[1]
    columns = pl.ds(pl.multiple_of(info[0] * width, HEAD), width)
    for index, block in enumerate(blocks):
        place = pl.ds(pl.multiple_of(info[index] * own_rows, ROWS), own_rows)
        own_ref[place, :] = block[:, columns]
        if index < EARLY:
            band = slice(index * own_rows, (index + 1) * own_rows)
            q_ref[place, :] = early_ref[0, band, :]
            kv_ref[0, place, :] = early_ref[1, band, :]
            kv_ref[1, place, :] = early_ref[2, band, :]
        else:
            band = slice((index - EARLY) * own_rows, (index - EARLY + 1) * own_rows)
            q_ref[place, :] = found[0][band]
            kv_ref[0, place, :] = found[1][band]
            kv_ref[1, place, :] = found[2][band]


def project_rows(blocks, info, mod_rows, weights):
    full, inner = weights.shape[1:]
    own_rows = blocks[0].shape[0]
    rows = own_rows * GROUP
    scratch = lambda count: (
        [pltpu.VMEM((count * own_rows, HEAD), jnp.float32)] * 2
        + [pltpu.VMEM((count * own_rows, full // CHUNKS), jnp.bfloat16)] * CHUNKS
    )
    early = local_call(
        rows_early_kernel,
        "rows_early",
        info,
        [*blocks[:EARLY], mod_rows, weights],
        [((3, EARLY * own_rows, inner), jnp.bfloat16)],
        scratch(EARLY),
        flops=6 * EARLY * own_rows * full * inner,
        moved=6 * full * inner,
    )[0]
    return local_call(
        rows_late_kernel,
        "rows_late",
        info,
        [*blocks, mod_rows, weights, early],
        [
            ((rows, inner), jnp.bfloat16),
            ((2, rows, inner), jnp.bfloat16),
            ((rows, full // GROUP), jnp.bfloat16),
        ],
        scratch(GROUP - EARLY),
        flops=6 * (GROUP - EARLY) * own_rows * full * inner,
        moved=6 * full * inner,
    )


def moments_kernel(info, *refs):
    del info
    blocks, out_ref = refs[:EARLY], refs[EARLY]
    rows = blocks[0].shape[0]

    for low in range(0, rows, BAND):
        band = slice(low, low + BAND)
        parts = [block[band, :].astype(jnp.float32) for block in blocks]
        pivot = jnp.mean(parts[0], axis=-1, keepdims=True)
        out_ref[0, band, :] = jnp.broadcast_to(pivot, (BAND, HEAD))
        out_ref[1, band, :], out_ref[2, band, :] = moments(parts, pivot)


def chunk_weight(info, w_ref):
    width = w_ref.shape[1] // GROUP
    each = GROUP // CHUNKS

    def weight(which, chunk):
        firsts = [info[chunk * each + part] * width for part in range(each)]
        return jnp.concatenate(
            [w_ref[which, pl.ds(pl.multiple_of(first, HEAD), width), :] for first in firsts],
            axis=0,
        )

    return weight


def queries_kernel(info, *refs):
    chunks, (w_ref, q_ref) = refs[:CHUNKS], refs[CHUNKS:]
    q_ref[...] = head_normed(products(lambda chunk: None, chunks, chunk_weight(info, w_ref), (0,))[0])


def columns_kernel(info, *refs):
    blocks, rest = refs[:GROUP], refs[GROUP:]
    mod_ref, w_ref, early_ref, kv_ref, chunks = *rest[:4], rest[4 : 4 + CHUNKS]
    mean_ref, factor_ref = rest[4 + CHUNKS :]
    rows, width = blocks[0].shape
    full = width * GROUP
    each = GROUP // CHUNKS

    for low in range(0, rows, BAND):
        band = slice(low, low + BAND)
        pivot = early_ref[0, band, :1]
        first, second = moments(
            [block[band, :].astype(jnp.float32) for block in blocks[EARLY:]], pivot
        )
        keep_moments(
            mean_ref,
            factor_ref,
            band,
            pivot,
            first + early_ref[1, band, :],
            second + early_ref[2, band, :],
            full,
        )

    place = lambda index: pl.ds(pl.multiple_of(info[index] * width, HEAD), width)

    def norm(chunk):
        for part in range(each):
            index = chunk * each + part
            chunks[chunk][:, part * width : (part + 1) * width] = normed(
                blocks[index][...], mean_ref[:, :1], factor_ref[:, :1], mod_ref, place(index)
            )

    totals = products(norm, chunks, chunk_weight(info, w_ref), (1, 2))
    kv_ref[0] = head_normed(totals[1])
    kv_ref[1] = totals[2].astype(jnp.bfloat16)


def project_columns(blocks, info, mod_rows, weights):
    full, inner = weights.shape[1:]
    rows = blocks[0].shape[0]
    early = local_call(
        moments_kernel,
        "moments",
        info,
        blocks[:EARLY],
        [((3, rows, HEAD), jnp.float32)],
        flops=rows * full,
        moved=2 * EARLY * blocks[0].size,
    )[0]
    kv, *chunks = local_call(
        columns_kernel,
        "columns",
        info,
        [*blocks, mod_rows, weights, early],
        [((2, rows, inner), jnp.bfloat16)] + [((rows, full // CHUNKS), jnp.bfloat16)] * CHUNKS,
        [pltpu.VMEM((rows, HEAD), jnp.float32)] * 2,
        flops=4 * rows * full * inner,
        moved=4 * full * inner,
    )
    (q,) = local_call(
        queries_kernel,
        "queries",
        info,
        [*chunks, weights],
        [((rows, inner), jnp.bfloat16)],
        flops=2 * rows * full * inner,
        moved=2 * full * inner,
    )
    return q, kv


def add_pair(query, kv, total_ref):
    factor = math.log2(math.e) / math.sqrt(HEAD)
    heads = [slice(low, low + HEAD) for low in range(0, query.shape[1], HEAD)]
    weights = []
    for cut in heads:
        scores = lax.dot_general(
            query[:, cut],
            kv[0, :, cut],
            (((1,), (1,)), ((), ())),
            preferred_element_type=jnp.float32,
        )
        weights.append(jnp.exp2(scores * factor).astype(jnp.bfloat16))
    for head, cut in enumerate(heads):
        values = kv[1, :, cut]
        total_ref[head] += jnp.dot(
            weights[head],
            jnp.concatenate([values, jnp.ones_like(values)], axis=1),
            preferred_element_type=jnp.float32,
        )


def attend_kernel(frames, info, *refs):
    count = len(frames)
    queries, kvs, rest = refs[:count], refs[count : count + 4], refs[count + 4 :]
    outs = rest[-4:-2] if frames[0] == 0 else rest[-2 - count : -2]
    mark_ref, total = rest[-2:]
    mark_ref[...] = jnp.zeros_like(mark_ref)
    rows, inner = queries[0].shape
    heads = inner // HEAD
    lanes = lax.broadcasted_iota(jnp.int32, (rows, HEAD), 1)
    for index, frame in enumerate(frames):
        total[...] = jnp.zeros_like(total)
        for which, kv in enumerate(kvs):

            @pl.when(info[4 + which] <= info[frame])
            def _(index=index, kv=kv):
                add_pair(queries[index], kv, total)

        sums = jnp.zeros((rows, HEAD), jnp.float32)
        for head in range(heads):
            cut = slice(head * HEAD, (head + 1) * HEAD)
            numerator, row_total = total[head, :, :HEAD], total[head, :, HEAD:]
            if frame == 0:
                outs[0][:, cut] = numerator
                sums = jnp.where(lanes == head, row_total, sums)
            else:
                outs[index][:rows, cut] = numerator.astype(jnp.bfloat16)
                coarse = row_total.astype(jnp.bfloat16).astype(jnp.float32)
                sums = jnp.where(lanes == head, coarse, sums)
                sums = jnp.where(lanes == heads + head, row_total - coarse, sums)
        if frame == 0:
            outs[1][...] = sums
        else:
            outs[index][rows:, :] = sums.T[:ROWS].astype(jnp.bfloat16)


def attend(frames, queries, kvs, info, after=()):
    rows, inner = queries[0].shape
    outs = (
        [((rows, inner), jnp.float32), ((rows, HEAD), jnp.float32)]
        if frames[0] == 0
        else [((rows + ROWS, inner), jnp.bfloat16)] * len(frames)
    )
    return local_call(
        functools.partial(attend_kernel, frames),
        "attend",
        info,
        [*(queries[frame] for frame in frames), *kvs, *after],
        outs + [((8, HEAD), jnp.float32)],
        [pltpu.VMEM((inner // HEAD, rows, 2 * HEAD), jnp.float32)],
        limit=8,
        flops=16 * len(frames) * rows * rows * inner,
        moved=32 * rows * inner,
    )


def finish_kernel(info, own_ref, own_sum_ref, *refs):
    del info
    got, out_ref = refs[:3], refs[3]
    rows, inner = own_ref.shape
    heads = inner // HEAD
    pairs = sum(ref[rows:, :].astype(jnp.float32) for ref in got)
    pairs = jnp.concatenate([pairs, jnp.zeros((HEAD - ROWS, inner), jnp.float32)], axis=0).T
    for head in range(heads):
        cut = slice(head * HEAD, (head + 1) * HEAD)
        row_total = (
            own_sum_ref[:, head : head + 1]
            + pairs[:, head : head + 1]
            + pairs[:, heads + head : heads + head + 1]
        )
        numerator = own_ref[:, cut] + sum(ref[:rows, cut].astype(jnp.float32) for ref in got)
        out_ref[:, cut] = (numerator / row_total).astype(jnp.bfloat16)


def finish(own, own_sum, got, info):
    return local_call(
        finish_kernel,
        "finish",
        info,
        [own, own_sum, *got],
        [(own.shape, jnp.bfloat16)],
    )[0]


def early_kernel(info, *refs):
    parts, (w_ref, out_ref) = refs[:EARLY], refs[EARLY:]
    out_ref[...] = sum(
        jnp.dot(part[...], w_ref[info[index]], preferred_element_type=jnp.float32)
        for index, part in enumerate(parts)
    )


def late_kernel(info, *refs):
    count = GROUP - EARLY
    parts, (sum_ref, w_ref, hidden_ref, mod_ref, out_ref) = refs[:count], refs[count:]
    width = hidden_ref.shape[1]
    total = sum_ref[...] + sum(
        jnp.dot(part[...], w_ref[info[EARLY + index]], preferred_element_type=jnp.float32)
        for index, part in enumerate(parts)
    )
    columns = pl.ds(pl.multiple_of(info[0] * width, HEAD), width)
    out_ref[...] = (hidden_ref[...].astype(jnp.float32) + mod_ref[2:3, columns] * total).astype(
        jnp.bfloat16
    )


def add_branch(parts, weights, hidden, mod_rows, info):
    rows, inner = parts[0].shape
    each = 2 * rows * inner * hidden.shape[1]
    moved = 4 * hidden.size
    early = local_call(
        early_kernel,
        "early",
        info,
        [*parts[:EARLY], weights],
        [(hidden.shape, jnp.float32)],
        flops=EARLY * each,
        moved=moved,
    )[0]
    return local_call(
        late_kernel,
        "late",
        info,
        [*parts[EARLY:], early, weights, hidden, mod_rows],
        [(hidden.shape, jnp.bfloat16)],
        flops=(GROUP - EARLY) * each,
        moved=moved,
    )[0]


def out_pieces(out_weight, core):
    rows, width = out_weight.shape
    half = rows // 2
    own = lax.dynamic_slice(out_weight, (core * half, 0), (half, width))
    return jnp.transpose(own.reshape(half, GROUP, width // GROUP), (1, 0, 2))


def out_columns(mine, core):
    theirs = over_frame(mine, lambda f: f ^ 1)
    first = core == 0
    return jnp.concatenate(
        [jnp.where(first, mine, theirs), jnp.where(first, theirs, mine)], axis=1
    )


def per_device(tokens, qkv_weight, out_weight, mod_table, levels, frame_order):
    own_rows, width = tokens.shape
    frame = lax.axis_index("frame")
    ids = jnp.arange(FRAMES, dtype=jnp.int32)
    level = jnp.sum(jnp.where(ids == frame, levels, 0))
    where = origins(lax.axis_index("dp")).astype(jnp.int32)
    shift = np.array([0, 12, 4, 8, 0, 0, 0, 0], np.int32)
    swap = np.array([0, 0, 0, 0, 0, 1, 2, 3], np.int32)
    others = ((frame + shift) % FRAMES) ^ swap
    ranks = jnp.sum(jnp.where(others[:, None] == ids[None, :], frame_order[None, :], 0), axis=1)
    chosen = [
        lax.dynamic_index_in_dim(mod_table, level + step, 0, keepdims=False)
        for step in range(STEPS)
    ]
    core = frame % 2
    blocks = gathered(tokens)
    source, blocks[4] = lax.optimization_barrier((jnp.transpose(qkv_weight, (1, 0, 2)), blocks[4]))
    weights = load(source, where)
    out_own, blocks[4] = lax.optimization_barrier((out_pieces(out_weight, core), blocks[4]))
    own_hidden = None
    out_weights = None
    attended = None
    for step_index in range(STEPS):
        mod_rows = chosen[step_index]
        if step_index == 0:
            q, kv, own_hidden = project_rows(blocks, where, mod_rows, weights)
        else:
            q, kv = project_columns(blocks, where, mod_rows, weights)
        queries = [
            q,
            over_frame(q, lambda f: f + 4),
            over_frame(q, lambda f: f - 4),
            over_frame(q, lambda f: f + 8),
        ]
        beside = over_frame(kv, lambda f: f ^ 2)
        mate = over_frame(kv, lambda f: f ^ 1)
        beside, queries[1], queries[2], queries[3], out_own = lax.optimization_barrier(
            (beside, queries[1], queries[2], queries[3], out_own)
        )
        if step_index == 0:
            out_mine = lax.all_to_all(out_own, "dp", 0, 0, tiled=True)
            out_own = level
        beside_mate = over_frame(beside, lambda f: f ^ 1)
        kvs = [kv, mate, beside, beside_mate]
        far, mark = attend([3], queries, kvs, ranks)
        chain = step_index == 0
        own, own_sum, mark = attend([0], queries, kvs, ranks, [mark] * chain)
        low, high, _ = attend([1, 2], queries, kvs, ranks, [mark] * chain)
        got = [
            over_frame(far, lambda f: f + 8),
            over_frame(low, lambda f: f - 4),
            over_frame(high, lambda f: f + 4),
        ]
        if step_index == 0:
            out_mine, got = lax.optimization_barrier((out_mine, got))
            out_weights = out_columns(out_mine, core)
        attended = finish(own, own_sum, got, where)
        own_hidden = add_branch(gathered(attended), out_weights, own_hidden, mod_rows, where)
        if step_index < STEPS - 1:
            blocks = gathered(own_hidden)
    pieces = own_hidden.reshape(GROUP, own_rows, width // GROUP)
    pieces = lax.all_to_all(pieces, "dp", 0, 0, tiled=True)
    hidden = jnp.transpose(pieces, (1, 0, 2)).reshape(own_rows, width)
    return (hidden, attended)


def solution(mesh):
    return jax.shard_map(
        per_device,
        mesh=mesh,
        in_specs=(P(("frame", "dp"), None), P(None, None, "dp"), P("dp", None), P(), P(), P()),
        out_specs=(P(("frame", "dp"), None), P("frame", "dp")),
        check_vma=False,
    )
```

```python
import functools
import math

import jax
import jax.numpy as jnp
import numpy as np
from jax import lax
from jax.experimental import pallas as pl
from jax.experimental.pallas import tpu as pltpu
from jax.sharding import PartitionSpec as P

HEAD = 128
STEPS = 2
EPSILON = 1e-06
ROWS = 16
BAND = 96
GROUP = 8
FRAMES = 16


def over_dp(value, to):
    return lax.ppermute(value, "dp", [(d, to(d) % GROUP) for d in range(GROUP)])


def over_frame(value, to):
    return lax.ppermute(value, "frame", [(f, to(f) % FRAMES) for f in range(FRAMES)])


def gathered(block):
    beside = over_dp(block, lambda d: d ^ 1)
    below = over_dp(block, lambda d: d + 2)
    above = over_dp(block, lambda d: d - 2)
    across = over_dp(block, lambda d: d + 4)
    beside_below = over_dp(beside, lambda d: d + 2)
    beside_above = over_dp(beside, lambda d: d - 2)
    beside_across = over_dp(across, lambda d: d ^ 1)
    return [block, beside, below, above, across, beside_below, beside_above, beside_across]


def origins(d):
    swap = np.array([0, 1, 0, 0, 0, 1, 1, 1], np.int32)
    shift = np.array([0, 0, 6, 2, 4, 6, 2, 4], np.int32)
    return ((d ^ swap) + shift) % GROUP


CHUNKS = 4


def local_call(kernel, name, info, operands, outs, scratch=(), limit=16, flops=0, moved=0):
    placed = [pltpu.with_memory_space_constraint(value, pltpu.VMEM) for value in operands]
    in_vmem = pl.BlockSpec(memory_space=pltpu.VMEM)
    return pl.pallas_call(
        kernel,
        out_shape=[pltpu.VMEM(shape, kind) for shape, kind in outs],
        in_specs=[pl.BlockSpec(memory_space=pltpu.SMEM)] + [in_vmem] * len(operands),
        out_specs=[in_vmem] * len(outs),
        scratch_shapes=list(scratch),
        compiler_params=pltpu.CompilerParams(vmem_limit_bytes=limit * 1024 * 1024),
        cost_estimate=pl.CostEstimate(flops=flops, bytes_accessed=moved, transcendentals=0),
        name=name,
    )(info, *placed)


def load_kernel(info, source, target, sems):
    del info
    copies = []
    for part in range(GROUP):
        span = source.shape[1] // GROUP
        cut = pl.ds(part * span, span)
        copies.append(
            pltpu.make_async_copy(source.at[:, cut, :], target.at[:, cut, :], sems.at[part])
        )
        copies[-1].start()
    for copy in copies:
        copy.wait()


def load(weights, info):
    return pl.pallas_call(
        load_kernel,
        out_shape=pltpu.VMEM(weights.shape, weights.dtype),
        in_specs=[pl.BlockSpec(memory_space=pltpu.SMEM), pl.BlockSpec(memory_space=pl.ANY)],
        out_specs=pl.BlockSpec(memory_space=pltpu.VMEM),
        scratch_shapes=[pltpu.SemaphoreType.DMA((GROUP,))],
        compiler_params=pltpu.CompilerParams(vmem_limit_bytes=2 * 1024 * 1024),
        cost_estimate=pl.CostEstimate(flops=0, bytes_accessed=2 * weights.size, transcendentals=0),
        name="load",
    )(info, pltpu.with_memory_space_constraint(weights, pltpu.HBM))


EARLY = 5


def folded(values):
    return sum(values[:, low : low + HEAD] for low in range(0, values.shape[1], HEAD))


def moments(parts, pivot):
    shifted = [part - pivot for part in parts]
    return folded(sum(shifted)), folded(sum(part * part for part in shifted))


def keep_moments(mean_ref, factor_ref, band, pivot, first, second, full):
    first = jnp.sum(first, axis=-1, keepdims=True) / full
    second = jnp.sum(second, axis=-1, keepdims=True) / full
    variance = second - first * first
    shape = (variance.shape[0], HEAD)
    mean_ref[band, :] = jnp.broadcast_to(pivot + first, shape)
    factor_ref[band, :] = jnp.broadcast_to(lax.rsqrt(variance + EPSILON), shape)


def normed(values, mean, factor, mod_ref, place):
    centered = values.astype(jnp.float32) - mean
    return (centered * factor * (1.0 + mod_ref[1:2, place]) + mod_ref[0:1, place]).astype(
        jnp.bfloat16
    )


def products(norm, chunks, weight, wanted=(0, 1, 2)):
    norm(0)
    totals = [None] * 3
    for chunk in range(CHUNKS):
        if chunk + 1 < CHUNKS:
            norm(chunk + 1)
        for which in wanted:
            term = jnp.dot(
                chunks[chunk][...], weight(which, chunk), preferred_element_type=jnp.float32
            )
            totals[which] = term if chunk == 0 else totals[which] + term
    return totals


def head_normed(values):
    blocks = []
    for low in range(0, values.shape[1], HEAD):
        block = values[:, low : low + HEAD]
        blocks.append(
            block * lax.rsqrt(jnp.mean(block * block, axis=-1, keepdims=True) + EPSILON)
        )
    return jnp.concatenate(blocks, axis=1).astype(jnp.bfloat16)


def rows_projected(blocks, mod_ref, w_ref, mean_ref, factor_ref, chunks):
    own_rows, full = blocks[0].shape
    width = full // GROUP
    span = full // CHUNKS
    for index, block in enumerate(blocks):
        rows = block[...].astype(jnp.float32)
        parts = [rows[:, chunk * width : (chunk + 1) * width] for chunk in range(GROUP)]
        pivot = jnp.mean(parts[0], axis=-1, keepdims=True)
        keep_moments(
            mean_ref,
            factor_ref,
            slice(index * own_rows, (index + 1) * own_rows),
            pivot,
            *moments(parts, pivot),
            full,
        )

    def norm(chunk):
        cut = slice(chunk * span, (chunk + 1) * span)
        for index, block in enumerate(blocks):
            band = slice(index * own_rows, (index + 1) * own_rows)
            chunks[chunk][band, :] = normed(
                block[:, cut], mean_ref[band, :1], factor_ref[band, :1], mod_ref, cut
            )

    totals = products(
        norm, chunks, lambda which, chunk: w_ref[which, chunk * span : (chunk + 1) * span, :]
    )
    return head_normed(totals[0]), head_normed(totals[1]), totals[2].astype(jnp.bfloat16)


def rows_early_kernel(info, *refs):
    del info
    blocks, (mod_ref, w_ref, out_ref, mean_ref, factor_ref) = refs[:EARLY], refs[EARLY:-CHUNKS]
    found = rows_projected(blocks, mod_ref, w_ref, mean_ref, factor_ref, refs[-CHUNKS:])
    for which in range(3):
        out_ref[which] = found[which]


def rows_late_kernel(info, *refs):
    blocks, rest = refs[:GROUP], refs[GROUP:-CHUNKS]
    mod_ref, w_ref, early_ref, q_ref, kv_ref, own_ref, mean_ref, factor_ref = rest
    found = rows_projected(blocks[EARLY:], mod_ref, w_ref, mean_ref, factor_ref, refs[-CHUNKS:])
    own_rows = blocks[0].shape[0]
    width = own_ref.shape[1]
    columns = pl.ds(pl.multiple_of(info[0] * width, HEAD), width)
    for index, block in enumerate(blocks):
        place = pl.ds(pl.multiple_of(info[index] * own_rows, ROWS), own_rows)
        own_ref[place, :] = block[:, columns]
        if index < EARLY:
            band = slice(index * own_rows, (index + 1) * own_rows)
            q_ref[place, :] = early_ref[0, band, :]
            kv_ref[0, place, :] = early_ref[1, band, :]
            kv_ref[1, place, :] = early_ref[2, band, :]
        else:
            band = slice((index - EARLY) * own_rows, (index - EARLY + 1) * own_rows)
            q_ref[place, :] = found[0][band]
            kv_ref[0, place, :] = found[1][band]
            kv_ref[1, place, :] = found[2][band]


def project_rows(blocks, info, mod_rows, weights):
    full, inner = weights.shape[1:]
    own_rows = blocks[0].shape[0]
    rows = own_rows * GROUP
    scratch = lambda count: (
        [pltpu.VMEM((count * own_rows, HEAD), jnp.float32)] * 2
        + [pltpu.VMEM((count * own_rows, full // CHUNKS), jnp.bfloat16)] * CHUNKS
    )
    early = local_call(
        rows_early_kernel,
        "rows_early",
        info,
        [*blocks[:EARLY], mod_rows, weights],
        [((3, EARLY * own_rows, inner), jnp.bfloat16)],
        scratch(EARLY),
        flops=6 * EARLY * own_rows * full * inner,
        moved=6 * full * inner,
    )[0]
    return local_call(
        rows_late_kernel,
        "rows_late",
        info,
        [*blocks, mod_rows, weights, early],
        [
            ((rows, inner), jnp.bfloat16),
            ((2, rows, inner), jnp.bfloat16),
            ((rows, full // GROUP), jnp.bfloat16),
        ],
        scratch(GROUP - EARLY),
        flops=6 * (GROUP - EARLY) * own_rows * full * inner,
        moved=6 * full * inner,
    )


def moments_kernel(info, *refs):
    del info
    blocks, out_ref = refs[:EARLY], refs[EARLY]
    rows = blocks[0].shape[0]

    for low in range(0, rows, BAND):
        band = slice(low, low + BAND)
        parts = [block[band, :].astype(jnp.float32) for block in blocks]
        pivot = jnp.mean(parts[0], axis=-1, keepdims=True)
        out_ref[0, band, :] = jnp.broadcast_to(pivot, (BAND, HEAD))
        out_ref[1, band, :], out_ref[2, band, :] = moments(parts, pivot)


def chunk_weight(info, w_ref):
    width = w_ref.shape[1] // GROUP
    each = GROUP // CHUNKS

    def weight(which, chunk):
        firsts = [info[chunk * each + part] * width for part in range(each)]
        return jnp.concatenate(
            [w_ref[which, pl.ds(pl.multiple_of(first, HEAD), width), :] for first in firsts],
            axis=0,
        )

    return weight


def queries_kernel(info, *refs):
    chunks, (w_ref, q_ref) = refs[:CHUNKS], refs[CHUNKS:]
    q_ref[...] = head_normed(products(lambda chunk: None, chunks, chunk_weight(info, w_ref), (0,))[0])


def columns_kernel(info, *refs):
    blocks, rest = refs[:GROUP], refs[GROUP:]
    mod_ref, w_ref, early_ref, kv_ref, chunks = *rest[:4], rest[4 : 4 + CHUNKS]
    mean_ref, factor_ref = rest[4 + CHUNKS :]
    rows, width = blocks[0].shape
    full = width * GROUP
    each = GROUP // CHUNKS

    for low in range(0, rows, BAND):
        band = slice(low, low + BAND)
        pivot = early_ref[0, band, :1]
        first, second = moments(
            [block[band, :].astype(jnp.float32) for block in blocks[EARLY:]], pivot
        )
        keep_moments(
            mean_ref,
            factor_ref,
            band,
            pivot,
            first + early_ref[1, band, :],
            second + early_ref[2, band, :],
            full,
        )

    place = lambda index: pl.ds(pl.multiple_of(info[index] * width, HEAD), width)

    def norm(chunk):
        for part in range(each):
            index = chunk * each + part
            chunks[chunk][:, part * width : (part + 1) * width] = normed(
                blocks[index][...], mean_ref[:, :1], factor_ref[:, :1], mod_ref, place(index)
            )

    totals = products(norm, chunks, chunk_weight(info, w_ref), (1, 2))
    kv_ref[0] = head_normed(totals[1])
    kv_ref[1] = totals[2].astype(jnp.bfloat16)


def project_columns(blocks, info, mod_rows, weights):
    full, inner = weights.shape[1:]
    rows = blocks[0].shape[0]
    early = local_call(
        moments_kernel,
        "moments",
        info,
        blocks[:EARLY],
        [((3, rows, HEAD), jnp.float32)],
        flops=rows * full,
        moved=2 * EARLY * blocks[0].size,
    )[0]
    kv, *chunks = local_call(
        columns_kernel,
        "columns",
        info,
        [*blocks, mod_rows, weights, early],
        [((2, rows, inner), jnp.bfloat16)] + [((rows, full // CHUNKS), jnp.bfloat16)] * CHUNKS,
        [pltpu.VMEM((rows, HEAD), jnp.float32)] * 2,
        flops=4 * rows * full * inner,
        moved=4 * full * inner,
    )
    (q,) = local_call(
        queries_kernel,
        "queries",
        info,
        [*chunks, weights],
        [((rows, inner), jnp.bfloat16)],
        flops=2 * rows * full * inner,
        moved=2 * full * inner,
    )
    return q, kv


def add_pair(query, kv, total_ref):
    factor = math.log2(math.e) / math.sqrt(HEAD)
    heads = [slice(low, low + HEAD) for low in range(0, query.shape[1], HEAD)]
    weights = []
    for cut in heads:
        scores = lax.dot_general(
            query[:, cut],
            kv[0, :, cut],
            (((1,), (1,)), ((), ())),
            preferred_element_type=jnp.float32,
        )
        weights.append(jnp.exp2(scores * factor).astype(jnp.bfloat16))
    for head, cut in enumerate(heads):
        values = kv[1, :, cut]
        total_ref[head] += jnp.dot(
            weights[head],
            jnp.concatenate([values, jnp.ones_like(values)], axis=1),
            preferred_element_type=jnp.float32,
        )


def attend_kernel(frames, info, *refs):
    count = len(frames)
    queries, kvs, rest = refs[:count], refs[count : count + 4], refs[count + 4 :]
    outs = rest[-4:-2] if frames[0] == 0 else rest[-2 - count : -2]
    mark_ref, total = rest[-2:]
    mark_ref[...] = jnp.zeros_like(mark_ref)
    rows, inner = queries[0].shape
    heads = inner // HEAD
    lanes = lax.broadcasted_iota(jnp.int32, (rows, HEAD), 1)
    for index, frame in enumerate(frames):
        total[...] = jnp.zeros_like(total)
        for which, kv in enumerate(kvs):

            @pl.when(info[4 + which] <= info[frame])
            def _(index=index, kv=kv):
                add_pair(queries[index], kv, total)

        sums = jnp.zeros((rows, HEAD), jnp.float32)
        for head in range(heads):
            cut = slice(head * HEAD, (head + 1) * HEAD)
            numerator, row_total = total[head, :, :HEAD], total[head, :, HEAD:]
            if frame == 0:
                outs[0][:, cut] = numerator
                sums = jnp.where(lanes == head, row_total, sums)
            else:
                outs[index][:rows, cut] = numerator.astype(jnp.bfloat16)
                coarse = row_total.astype(jnp.bfloat16).astype(jnp.float32)
                sums = jnp.where(lanes == head, coarse, sums)
                sums = jnp.where(lanes == heads + head, row_total - coarse, sums)
        if frame == 0:
            outs[1][...] = sums
        else:
            outs[index][rows:, :] = sums.T[:ROWS].astype(jnp.bfloat16)


def attend(frames, queries, kvs, info, after=()):
    rows, inner = queries[0].shape
    outs = (
        [((rows, inner), jnp.float32), ((rows, HEAD), jnp.float32)]
        if frames[0] == 0
        else [((rows + ROWS, inner), jnp.bfloat16)] * len(frames)
    )
    return local_call(
        functools.partial(attend_kernel, frames),
        "attend",
        info,
        [*(queries[frame] for frame in frames), *kvs, *after],
        outs + [((8, HEAD), jnp.float32)],
        [pltpu.VMEM((inner // HEAD, rows, 2 * HEAD), jnp.float32)],
        limit=8,
        flops=16 * len(frames) * rows * rows * inner,
        moved=32 * rows * inner,
    )


def finish_kernel(info, own_ref, own_sum_ref, *refs):
    del info
    got, out_ref = refs[:3], refs[3]
    rows, inner = own_ref.shape
    heads = inner // HEAD
    pairs = sum(ref[rows:, :].astype(jnp.float32) for ref in got)
    pairs = jnp.concatenate([pairs, jnp.zeros((HEAD - ROWS, inner), jnp.float32)], axis=0).T
    for head in range(heads):
        cut = slice(head * HEAD, (head + 1) * HEAD)
        row_total = (
            own_sum_ref[:, head : head + 1]
            + pairs[:, head : head + 1]
            + pairs[:, heads + head : heads + head + 1]
        )
        numerator = own_ref[:, cut] + sum(ref[:rows, cut].astype(jnp.float32) for ref in got)
        out_ref[:, cut] = (numerator / row_total).astype(jnp.bfloat16)


def finish(own, own_sum, got, info):
    return local_call(
        finish_kernel,
        "finish",
        info,
        [own, own_sum, *got],
        [(own.shape, jnp.bfloat16)],
    )[0]


def early_kernel(info, *refs):
    parts, (w_ref, out_ref) = refs[:EARLY], refs[EARLY:]
    out_ref[...] = sum(
        jnp.dot(part[...], w_ref[info[index]], preferred_element_type=jnp.float32)
        for index, part in enumerate(parts)
    )


def late_kernel(info, *refs):
    count = GROUP - EARLY
    parts, (sum_ref, w_ref, hidden_ref, mod_ref, out_ref) = refs[:count], refs[count:]
    width = hidden_ref.shape[1]
    total = sum_ref[...] + sum(
        jnp.dot(part[...], w_ref[info[EARLY + index]], preferred_element_type=jnp.float32)
        for index, part in enumerate(parts)
    )
    columns = pl.ds(pl.multiple_of(info[0] * width, HEAD), width)
    out_ref[...] = (hidden_ref[...].astype(jnp.float32) + mod_ref[2:3, columns] * total).astype(
        jnp.bfloat16
    )


def add_branch(parts, weights, hidden, mod_rows, info):
    rows, inner = parts[0].shape
    each = 2 * rows * inner * hidden.shape[1]
    moved = 4 * hidden.size
    early = local_call(
        early_kernel,
        "early",
        info,
        [*parts[:EARLY], weights],
        [(hidden.shape, jnp.float32)],
        flops=EARLY * each,
        moved=moved,
    )[0]
    return local_call(
        late_kernel,
        "late",
        info,
        [*parts[EARLY:], early, weights, hidden, mod_rows],
        [(hidden.shape, jnp.bfloat16)],
        flops=(GROUP - EARLY) * each,
        moved=moved,
    )[0]


def out_pieces(out_weight, core):
    rows, width = out_weight.shape
    half = rows // 2
    own = lax.dynamic_slice(out_weight, (core * half, 0), (half, width))
    return jnp.transpose(own.reshape(half, GROUP, width // GROUP), (1, 0, 2))


def out_columns(mine, core):
    theirs = over_frame(mine, lambda f: f ^ 1)
    first = core == 0
    return jnp.concatenate(
        [jnp.where(first, mine, theirs), jnp.where(first, theirs, mine)], axis=1
    )


def per_device(tokens, qkv_weight, out_weight, mod_table, levels, frame_order):
    own_rows, width = tokens.shape
    frame = lax.axis_index("frame")
    ids = jnp.arange(FRAMES, dtype=jnp.int32)
    level = jnp.sum(jnp.where(ids == frame, levels, 0))
    where = origins(lax.axis_index("dp")).astype(jnp.int32)
    shift = np.array([0, 12, 4, 8, 0, 0, 0, 0], np.int32)
    swap = np.array([0, 0, 0, 0, 0, 1, 2, 3], np.int32)
    others = ((frame + shift) % FRAMES) ^ swap
    ranks = jnp.sum(jnp.where(others[:, None] == ids[None, :], frame_order[None, :], 0), axis=1)
    chosen = [
        lax.dynamic_index_in_dim(mod_table, level + step, 0, keepdims=False)
        for step in range(STEPS)
    ]
    core = frame % 2
    blocks = gathered(tokens)
    source, blocks[4] = lax.optimization_barrier((jnp.transpose(qkv_weight, (1, 0, 2)), blocks[4]))
    weights = load(source, where)
    own_hidden = None
    out_weights = None
    attended = None
    for step_index in range(STEPS):
        mod_rows = chosen[step_index]
        if step_index == 0:
            q, kv, own_hidden = project_rows(blocks, where, mod_rows, weights)
            late_weight, own_hidden = lax.optimization_barrier((out_weight, own_hidden))
            out_own = out_pieces(late_weight, core)
        else:
            q, kv = project_columns(blocks, where, mod_rows, weights)
        queries = [
            q,
            over_frame(q, lambda f: f + 4),
            over_frame(q, lambda f: f - 4),
            over_frame(q, lambda f: f + 8),
        ]
        beside = over_frame(kv, lambda f: f ^ 2)
        mate = over_frame(kv, lambda f: f ^ 1)
        beside, queries[1], queries[2], queries[3], out_own = lax.optimization_barrier(
            (beside, queries[1], queries[2], queries[3], out_own)
        )
        if step_index == 0:
            out_mine = lax.all_to_all(out_own, "dp", 0, 0, tiled=True)
            out_own = level
        beside_mate = over_frame(beside, lambda f: f ^ 1)
        kvs = [kv, mate, beside, beside_mate]
        far, mark = attend([3], queries, kvs, ranks)
        chain = step_index == 0
        own, own_sum, mark = attend([0], queries, kvs, ranks, [mark] * chain)
        low, high, _ = attend([1, 2], queries, kvs, ranks, [mark] * chain)
        got = [
            over_frame(far, lambda f: f + 8),
            over_frame(low, lambda f: f - 4),
            over_frame(high, lambda f: f + 4),
        ]
        if step_index == 0:
            out_mine, got = lax.optimization_barrier((out_mine, got))
            out_weights = out_columns(out_mine, core)
        attended = finish(own, own_sum, got, where)
        own_hidden = add_branch(gathered(attended), out_weights, own_hidden, mod_rows, where)
        if step_index < STEPS - 1:
            blocks = gathered(own_hidden)
    pieces = own_hidden.reshape(GROUP, own_rows, width // GROUP)
    pieces = lax.all_to_all(pieces, "dp", 0, 0, tiled=True)
    hidden = jnp.transpose(pieces, (1, 0, 2)).reshape(own_rows, width)
    return (hidden, attended)


def solution(mesh):
    return jax.shard_map(
        per_device,
        mesh=mesh,
        in_specs=(P(("frame", "dp"), None), P(None, None, "dp"), P("dp", None), P(), P(), P()),
        out_specs=(P(("frame", "dp"), None), P("frame", "dp")),
        check_vma=False,
    )
```

```python
import functools
import math

import jax
import jax.numpy as jnp
import numpy as np
from jax import lax
from jax.experimental import pallas as pl
from jax.experimental.pallas import tpu as pltpu
from jax.sharding import PartitionSpec as P

HEAD = 128
STEPS = 2
EPSILON = 1e-06
ROWS = 16
BAND = 96
GROUP = 8
FRAMES = 16


def over_dp(value, to):
    return lax.ppermute(value, "dp", [(d, to(d) % GROUP) for d in range(GROUP)])


def over_frame(value, to):
    return lax.ppermute(value, "frame", [(f, to(f) % FRAMES) for f in range(FRAMES)])


def gathered(block):
    beside = over_dp(block, lambda d: d ^ 1)
    below = over_dp(block, lambda d: d + 2)
    above = over_dp(block, lambda d: d - 2)
    across = over_dp(block, lambda d: d + 4)
    beside_below = over_dp(beside, lambda d: d + 2)
    beside_above = over_dp(beside, lambda d: d - 2)
    beside_across = over_dp(across, lambda d: d ^ 1)
    return [block, beside, below, above, across, beside_below, beside_above, beside_across]


def origins(d):
    swap = np.array([0, 1, 0, 0, 0, 1, 1, 1], np.int32)
    shift = np.array([0, 0, 6, 2, 4, 6, 2, 4], np.int32)
    return ((d ^ swap) + shift) % GROUP


CHUNKS = 4


def local_call(kernel, name, info, operands, outs, scratch=(), limit=16, flops=0, moved=0):
    placed = [pltpu.with_memory_space_constraint(value, pltpu.VMEM) for value in operands]
    in_vmem = pl.BlockSpec(memory_space=pltpu.VMEM)
    return pl.pallas_call(
        kernel,
        out_shape=[pltpu.VMEM(shape, kind) for shape, kind in outs],
        in_specs=[pl.BlockSpec(memory_space=pltpu.SMEM)] + [in_vmem] * len(operands),
        out_specs=[in_vmem] * len(outs),
        scratch_shapes=list(scratch),
        compiler_params=pltpu.CompilerParams(vmem_limit_bytes=limit * 1024 * 1024),
        cost_estimate=pl.CostEstimate(flops=flops, bytes_accessed=moved, transcendentals=0),
        name=name,
    )(info, *placed)


def load_kernel(info, source, target, sems):
    del info
    copies = []
    for part in range(GROUP):
        span = source.shape[1] // GROUP
        cut = pl.ds(part * span, span)
        copies.append(
            pltpu.make_async_copy(source.at[:, cut, :], target.at[:, cut, :], sems.at[part])
        )
        copies[-1].start()
    for copy in copies:
        copy.wait()


def load(weights, info):
    return pl.pallas_call(
        load_kernel,
        out_shape=pltpu.VMEM(weights.shape, weights.dtype),
        in_specs=[pl.BlockSpec(memory_space=pltpu.SMEM), pl.BlockSpec(memory_space=pl.ANY)],
        out_specs=pl.BlockSpec(memory_space=pltpu.VMEM),
        scratch_shapes=[pltpu.SemaphoreType.DMA((GROUP,))],
        compiler_params=pltpu.CompilerParams(vmem_limit_bytes=2 * 1024 * 1024),
        cost_estimate=pl.CostEstimate(flops=0, bytes_accessed=2 * weights.size, transcendentals=0),
        name="load",
    )(info, pltpu.with_memory_space_constraint(weights, pltpu.HBM))


EARLY = 5


def folded(values):
    return sum(values[:, low : low + HEAD] for low in range(0, values.shape[1], HEAD))


def moments(parts, pivot):
    shifted = [part - pivot for part in parts]
    return folded(sum(shifted)), folded(sum(part * part for part in shifted))


def keep_moments(mean_ref, factor_ref, band, pivot, first, second, full):
    first = jnp.sum(first, axis=-1, keepdims=True) / full
    second = jnp.sum(second, axis=-1, keepdims=True) / full
    variance = second - first * first
    shape = (variance.shape[0], HEAD)
    mean_ref[band, :] = jnp.broadcast_to(pivot + first, shape)
    factor_ref[band, :] = jnp.broadcast_to(lax.rsqrt(variance + EPSILON), shape)


def normed(values, mean, factor, mod_ref, place):
    centered = values.astype(jnp.float32) - mean
    return (centered * factor * (1.0 + mod_ref[1:2, place]) + mod_ref[0:1, place]).astype(
        jnp.bfloat16
    )


def products(norm, chunks, weight, wanted=(0, 1, 2)):
    norm(0)
    totals = [None] * 3
    for chunk in range(CHUNKS):
        if chunk + 1 < CHUNKS:
            norm(chunk + 1)
        for which in wanted:
            term = jnp.dot(
                chunks[chunk][...], weight(which, chunk), preferred_element_type=jnp.float32
            )
            totals[which] = term if chunk == 0 else totals[which] + term
    return totals


def head_normed(values):
    blocks = []
    for low in range(0, values.shape[1], HEAD):
        block = values[:, low : low + HEAD]
        blocks.append(
            block * lax.rsqrt(jnp.mean(block * block, axis=-1, keepdims=True) + EPSILON)
        )
    return jnp.concatenate(blocks, axis=1).astype(jnp.bfloat16)


def rows_projected(blocks, mod_ref, w_ref, mean_ref, factor_ref, chunks):
    own_rows, full = blocks[0].shape
    width = full // GROUP
    span = full // CHUNKS
    for index, block in enumerate(blocks):
        rows = block[...].astype(jnp.float32)
        parts = [rows[:, chunk * width : (chunk + 1) * width] for chunk in range(GROUP)]
        pivot = jnp.mean(parts[0], axis=-1, keepdims=True)
        keep_moments(
            mean_ref,
            factor_ref,
            slice(index * own_rows, (index + 1) * own_rows),
            pivot,
            *moments(parts, pivot),
            full,
        )

    def norm(chunk):
        cut = slice(chunk * span, (chunk + 1) * span)
        for index, block in enumerate(blocks):
            band = slice(index * own_rows, (index + 1) * own_rows)
            chunks[chunk][band, :] = normed(
                block[:, cut], mean_ref[band, :1], factor_ref[band, :1], mod_ref, cut
            )

    totals = products(
        norm, chunks, lambda which, chunk: w_ref[which, chunk * span : (chunk + 1) * span, :]
    )
    return head_normed(totals[0]), head_normed(totals[1]), totals[2].astype(jnp.bfloat16)


def rows_early_kernel(info, *refs):
    del info
    blocks, (mod_ref, w_ref, out_ref, mean_ref, factor_ref) = refs[:EARLY], refs[EARLY:-CHUNKS]
    found = rows_projected(blocks, mod_ref, w_ref, mean_ref, factor_ref, refs[-CHUNKS:])
    for which in range(3):
        out_ref[which] = found[which]


def rows_late_kernel(info, *refs):
    blocks, rest = refs[:GROUP], refs[GROUP:-CHUNKS]
    mod_ref, w_ref, early_ref, q_ref, kv_ref, own_ref, mean_ref, factor_ref = rest
    found = rows_projected(blocks[EARLY:], mod_ref, w_ref, mean_ref, factor_ref, refs[-CHUNKS:])
    own_rows = blocks[0].shape[0]
    width = own_ref.shape[1]
    columns = pl.ds(pl.multiple_of(info[0] * width, HEAD), width)
    for index, block in enumerate(blocks):
        place = pl.ds(pl.multiple_of(info[index] * own_rows, ROWS), own_rows)
        own_ref[place, :] = block[:, columns]
        if index < EARLY:
            band = slice(index * own_rows, (index + 1) * own_rows)
            q_ref[place, :] = early_ref[0, band, :]
            kv_ref[0, place, :] = early_ref[1, band, :]
            kv_ref[1, place, :] = early_ref[2, band, :]
        else:
            band = slice((index - EARLY) * own_rows, (index - EARLY + 1) * own_rows)
            q_ref[place, :] = found[0][band]
            kv_ref[0, place, :] = found[1][band]
            kv_ref[1, place, :] = found[2][band]


def project_rows(blocks, info, mod_rows, weights):
    full, inner = weights.shape[1:]
    own_rows = blocks[0].shape[0]
    rows = own_rows * GROUP
    scratch = lambda count: (
        [pltpu.VMEM((count * own_rows, HEAD), jnp.float32)] * 2
        + [pltpu.VMEM((count * own_rows, full // CHUNKS), jnp.bfloat16)] * CHUNKS
    )
    early = local_call(
        rows_early_kernel,
        "rows_early",
        info,
        [*blocks[:EARLY], mod_rows, weights],
        [((3, EARLY * own_rows, inner), jnp.bfloat16)],
        scratch(EARLY),
        flops=6 * EARLY * own_rows * full * inner,
        moved=6 * full * inner,
    )[0]
    return local_call(
        rows_late_kernel,
        "rows_late",
        info,
        [*blocks, mod_rows, weights, early],
        [
            ((rows, inner), jnp.bfloat16),
            ((2, rows, inner), jnp.bfloat16),
            ((rows, full // GROUP), jnp.bfloat16),
        ],
        scratch(GROUP - EARLY),
        flops=6 * (GROUP - EARLY) * own_rows * full * inner,
        moved=6 * full * inner,
    )


def moments_kernel(info, *refs):
    del info
    blocks, out_ref = refs[:EARLY], refs[EARLY]
    rows = blocks[0].shape[0]

    for low in range(0, rows, BAND):
        band = slice(low, low + BAND)
        parts = [block[band, :].astype(jnp.float32) for block in blocks]
        pivot = jnp.mean(parts[0], axis=-1, keepdims=True)
        out_ref[0, band, :] = jnp.broadcast_to(pivot, (BAND, HEAD))
        out_ref[1, band, :], out_ref[2, band, :] = moments(parts, pivot)


def chunk_weight(info, w_ref):
    width = w_ref.shape[1] // GROUP
    each = GROUP // CHUNKS

    def weight(which, chunk):
        firsts = [info[chunk * each + part] * width for part in range(each)]
        return jnp.concatenate(
            [w_ref[which, pl.ds(pl.multiple_of(first, HEAD), width), :] for first in firsts],
            axis=0,
        )

    return weight


def queries_kernel(info, *refs):
    chunks, (w_ref, q_ref) = refs[:CHUNKS], refs[CHUNKS:]
    q_ref[...] = head_normed(products(lambda chunk: None, chunks, chunk_weight(info, w_ref), (0,))[0])


def columns_kernel(info, *refs):
    blocks, rest = refs[:GROUP], refs[GROUP:]
    mod_ref, w_ref, early_ref, kv_ref, chunks = *rest[:4], rest[4 : 4 + CHUNKS]
    mean_ref, factor_ref = rest[4 + CHUNKS :]
    rows, width = blocks[0].shape
    full = width * GROUP
    each = GROUP // CHUNKS

    for low in range(0, rows, BAND):
        band = slice(low, low + BAND)
        pivot = early_ref[0, band, :1]
        first, second = moments(
            [block[band, :].astype(jnp.float32) for block in blocks[EARLY:]], pivot
        )
        keep_moments(
            mean_ref,
            factor_ref,
            band,
            pivot,
            first + early_ref[1, band, :],
            second + early_ref[2, band, :],
            full,
        )

    place = lambda index: pl.ds(pl.multiple_of(info[index] * width, HEAD), width)

    def norm(chunk):
        for part in range(each):
            index = chunk * each + part
            chunks[chunk][:, part * width : (part + 1) * width] = normed(
                blocks[index][...], mean_ref[:, :1], factor_ref[:, :1], mod_ref, place(index)
            )

    totals = products(norm, chunks, chunk_weight(info, w_ref), (1, 2))
    kv_ref[0] = head_normed(totals[1])
    kv_ref[1] = totals[2].astype(jnp.bfloat16)


def project_columns(blocks, info, mod_rows, weights):
    full, inner = weights.shape[1:]
    rows = blocks[0].shape[0]
    early = local_call(
        moments_kernel,
        "moments",
        info,
        blocks[:EARLY],
        [((3, rows, HEAD), jnp.float32)],
        flops=rows * full,
        moved=2 * EARLY * blocks[0].size,
    )[0]
    kv, *chunks = local_call(
        columns_kernel,
        "columns",
        info,
        [*blocks, mod_rows, weights, early],
        [((2, rows, inner), jnp.bfloat16)] + [((rows, full // CHUNKS), jnp.bfloat16)] * CHUNKS,
        [pltpu.VMEM((rows, HEAD), jnp.float32)] * 2,
        flops=4 * rows * full * inner,
        moved=4 * full * inner,
    )
    (q,) = local_call(
        queries_kernel,
        "queries",
        info,
        [*chunks, weights],
        [((rows, inner), jnp.bfloat16)],
        flops=2 * rows * full * inner,
        moved=2 * full * inner,
    )
    return q, kv


def add_pair(query, kv, total_ref):
    factor = math.log2(math.e) / math.sqrt(HEAD)
    heads = [slice(low, low + HEAD) for low in range(0, query.shape[1], HEAD)]
    weights = []
    for cut in heads:
        scores = lax.dot_general(
            query[:, cut],
            kv[0, :, cut],
            (((1,), (1,)), ((), ())),
            preferred_element_type=jnp.float32,
        )
        weights.append(jnp.exp2(scores * factor).astype(jnp.bfloat16))
    for head, cut in enumerate(heads):
        values = kv[1, :, cut]
        total_ref[head] += jnp.dot(
            weights[head],
            jnp.concatenate([values, jnp.ones_like(values)], axis=1),
            preferred_element_type=jnp.float32,
        )


def attend_kernel(frames, info, *refs):
    count = len(frames)
    queries, kvs, rest = refs[:count], refs[count : count + 4], refs[count + 4 :]
    outs = rest[-4:-2] if frames[0] == 0 else rest[-2 - count : -2]
    mark_ref, total = rest[-2:]
    mark_ref[...] = jnp.zeros_like(mark_ref)
    rows, inner = queries[0].shape
    heads = inner // HEAD
    lanes = lax.broadcasted_iota(jnp.int32, (rows, HEAD), 1)
    for index, frame in enumerate(frames):
        total[...] = jnp.zeros_like(total)
        for which, kv in enumerate(kvs):

            @pl.when(info[4 + which] <= info[frame])
            def _(index=index, kv=kv):
                add_pair(queries[index], kv, total)

        sums = jnp.zeros((rows, HEAD), jnp.float32)
        for head in range(heads):
            cut = slice(head * HEAD, (head + 1) * HEAD)
            numerator, row_total = total[head, :, :HEAD], total[head, :, HEAD:]
            if frame == 0:
                outs[0][:, cut] = numerator
                sums = jnp.where(lanes == head, row_total, sums)
            else:
                outs[index][:rows, cut] = numerator.astype(jnp.bfloat16)
                coarse = row_total.astype(jnp.bfloat16).astype(jnp.float32)
                sums = jnp.where(lanes == head, coarse, sums)
                sums = jnp.where(lanes == heads + head, row_total - coarse, sums)
        if frame == 0:
            outs[1][...] = sums
        else:
            outs[index][rows:, :] = sums.T[:ROWS].astype(jnp.bfloat16)


def attend(frames, queries, kvs, info, after=()):
    rows, inner = queries[0].shape
    outs = (
        [((rows, inner), jnp.float32), ((rows, HEAD), jnp.float32)]
        if frames[0] == 0
        else [((rows + ROWS, inner), jnp.bfloat16)] * len(frames)
    )
    return local_call(
        functools.partial(attend_kernel, frames),
        "attend",
        info,
        [*(queries[frame] for frame in frames), *kvs, *after],
        outs + [((8, HEAD), jnp.float32)],
        [pltpu.VMEM((inner // HEAD, rows, 2 * HEAD), jnp.float32)],
        limit=8,
        flops=16 * len(frames) * rows * rows * inner,
        moved=32 * rows * inner,
    )


def finish_kernel(info, own_ref, own_sum_ref, *refs):
    del info
    got, out_ref = refs[:3], refs[3]
    rows, inner = own_ref.shape
    heads = inner // HEAD
    pairs = sum(ref[rows:, :].astype(jnp.float32) for ref in got)
    pairs = jnp.concatenate([pairs, jnp.zeros((HEAD - ROWS, inner), jnp.float32)], axis=0).T
    for head in range(heads):
        cut = slice(head * HEAD, (head + 1) * HEAD)
        row_total = (
            own_sum_ref[:, head : head + 1]
            + pairs[:, head : head + 1]
            + pairs[:, heads + head : heads + head + 1]
        )
        numerator = own_ref[:, cut] + sum(ref[:rows, cut].astype(jnp.float32) for ref in got)
        out_ref[:, cut] = (numerator / row_total).astype(jnp.bfloat16)


def finish(own, own_sum, got, info):
    return local_call(
        finish_kernel,
        "finish",
        info,
        [own, own_sum, *got],
        [(own.shape, jnp.bfloat16)],
    )[0]


def early_kernel(info, *refs):
    parts, (w_ref, out_ref) = refs[:EARLY], refs[EARLY:]
    out_ref[...] = sum(
        jnp.dot(part[...], w_ref[info[index]], preferred_element_type=jnp.float32)
        for index, part in enumerate(parts)
    )


def late_kernel(info, *refs):
    count = GROUP - EARLY
    parts, (sum_ref, w_ref, hidden_ref, mod_ref, out_ref) = refs[:count], refs[count:]
    width = hidden_ref.shape[1]
    total = sum_ref[...] + sum(
        jnp.dot(part[...], w_ref[info[EARLY + index]], preferred_element_type=jnp.float32)
        for index, part in enumerate(parts)
    )
    columns = pl.ds(pl.multiple_of(info[0] * width, HEAD), width)
    out_ref[...] = (hidden_ref[...].astype(jnp.float32) + mod_ref[2:3, columns] * total).astype(
        jnp.bfloat16
    )


def add_branch(parts, weights, hidden, mod_rows, info):
    rows, inner = parts[0].shape
    each = 2 * rows * inner * hidden.shape[1]
    moved = 4 * hidden.size
    early = local_call(
        early_kernel,
        "early",
        info,
        [*parts[:EARLY], weights],
        [(hidden.shape, jnp.float32)],
        flops=EARLY * each,
        moved=moved,
    )[0]
    return local_call(
        late_kernel,
        "late",
        info,
        [*parts[EARLY:], early, weights, hidden, mod_rows],
        [(hidden.shape, jnp.bfloat16)],
        flops=(GROUP - EARLY) * each,
        moved=moved,
    )[0]


def out_pieces(out_weight, core):
    rows, width = out_weight.shape
    half = rows // 2
    own = lax.dynamic_slice(out_weight, (core * half, 0), (half, width))
    return jnp.transpose(own.reshape(half, GROUP, width // GROUP), (1, 0, 2))


def out_columns(mine, core):
    theirs = over_frame(mine, lambda f: f ^ 1)
    first = core == 0
    return jnp.concatenate(
        [jnp.where(first, mine, theirs), jnp.where(first, theirs, mine)], axis=1
    )


def per_device(tokens, qkv_weight, out_weight, mod_table, levels, frame_order):
    own_rows, width = tokens.shape
    frame = lax.axis_index("frame")
    ids = jnp.arange(FRAMES, dtype=jnp.int32)
    level = jnp.sum(jnp.where(ids == frame, levels, 0))
    where = origins(lax.axis_index("dp")).astype(jnp.int32)
    shift = np.array([0, 12, 4, 8, 0, 0, 0, 0], np.int32)
    swap = np.array([0, 0, 0, 0, 0, 1, 2, 3], np.int32)
    others = ((frame + shift) % FRAMES) ^ swap
    ranks = jnp.sum(jnp.where(others[:, None] == ids[None, :], frame_order[None, :], 0), axis=1)
    chosen = [
        lax.dynamic_index_in_dim(mod_table, level + step, 0, keepdims=False)
        for step in range(STEPS)
    ]
    core = frame % 2
    blocks = gathered(tokens)
    source, blocks[4] = lax.optimization_barrier((jnp.transpose(qkv_weight, (1, 0, 2)), blocks[4]))
    weights = load(source, where)
    own_hidden = None
    out_weights = None
    attended = None
    for step_index in range(STEPS):
        mod_rows = chosen[step_index]
        if step_index == 0:
            q, kv, own_hidden = project_rows(blocks, where, mod_rows, weights)
            late_weight, own_hidden = lax.optimization_barrier((out_weight, own_hidden))
            out_own = out_pieces(late_weight, core)
        else:
            q, kv = project_columns(blocks, where, mod_rows, weights)
        queries = [
            q,
            over_frame(q, lambda f: f + 4),
            over_frame(q, lambda f: f - 4),
            over_frame(q, lambda f: f + 8),
        ]
        beside = over_frame(kv, lambda f: f ^ 2)
        mate = over_frame(kv, lambda f: f ^ 1)
        beside, queries[1], queries[2], queries[3], out_own = lax.optimization_barrier(
            (beside, queries[1], queries[2], queries[3], out_own)
        )
        if step_index == 0:
            out_mine = lax.all_to_all(out_own, "dp", 0, 0, tiled=True)
            out_own = level
        beside_mate = over_frame(beside, lambda f: f ^ 1)
        kvs = [kv, mate, beside, beside_mate]
        far, mark = attend([3], queries, kvs, ranks)
        chain = True
        own, own_sum, mark = attend([0], queries, kvs, ranks, [mark] * chain)
        low, high, _ = attend([1, 2], queries, kvs, ranks, [mark] * chain)
        got = [
            over_frame(far, lambda f: f + 8),
            over_frame(low, lambda f: f - 4),
            over_frame(high, lambda f: f + 4),
        ]
        if step_index == 0:
            out_mine, got = lax.optimization_barrier((out_mine, got))
            out_weights = out_columns(out_mine, core)
        attended = finish(own, own_sum, got, where)
        own_hidden = add_branch(gathered(attended), out_weights, own_hidden, mod_rows, where)
        if step_index < STEPS - 1:
            blocks = gathered(own_hidden)
    pieces = own_hidden.reshape(GROUP, own_rows, width // GROUP)
    pieces = lax.all_to_all(pieces, "dp", 0, 0, tiled=True)
    hidden = jnp.transpose(pieces, (1, 0, 2)).reshape(own_rows, width)
    return (hidden, attended)


def solution(mesh):
    return jax.shard_map(
        per_device,
        mesh=mesh,
        in_specs=(P(("frame", "dp"), None), P(None, None, "dp"), P("dp", None), P(), P(), P()),
        out_specs=(P(("frame", "dp"), None), P("frame", "dp")),
        check_vma=False,
    )
```
